256 devices in a mesh: rep: 32 (over z, x), fsdp: 8 (over y, core).
Axes of the slice: x: 4, y: 4, z: 8, core: 2. Of those that a mesh axis runs over, the one named last changes fastest.
Arguments:
- acts: bfloat16 [32768, 8192], P(('rep', 'fsdp')), may hold values from -6 to 6
- grads_out: bfloat16 [32768, 2048], P(('rep', 'fsdp')), may hold values from -0.1875 to 0.1875
- error: bfloat16 [32, 2, 8192, 1024], P('rep', None, 'fsdp'), may hold values from -6 to 6
- warm_q: float32 [2, 32, 1024], replicated, may hold values from -6 to 6
Outputs:
- new_error: bfloat16 [32, 2, 8192, 1024], P('rep', None, 'fsdp')
- p_factor: float32 [2, 32, 8192], P(None, None, 'fsdp')
- q_factor: float32 [2, 32, 1024], replicated
The draws below stay inside these ranges and needn't reach their ends.
All inputs are finite; a program needn't handle non-finite values.
Results may differ from the reference program's by a relative error of at most 0.01.
Values may be sent and summed in bfloat16 or wider, within the bound.
No kernel may reach another device: no remote copies, remote signals or barrier semaphores. Data moves between devices by JAX's collectives and lax.ppermute only.
A program may use at most 128 MiB of HBM per device.

```python
import math
import jax
import jax.numpy as jnp
from jax import lax

D = 8192
KVDIM = 1024
RANK = 32
POWER = 2
TOK_DEV = 128
TOKENS = 32768
N_REP = 32
N_FSDP = 8


def block_levels(rng, dims, shards, smallest, largest):
    def one(axis_at, parts):
        steps = jax.random.uniform(jax.random.fold_in(jax.random.fold_in(rng, 6), axis_at), (parts,), jnp.float32, smallest / len(shards), largest / len(shards))
        return jnp.repeat(jnp.exp(steps), dims[axis_at] // parts).reshape((-1,) + (1,) * (len(dims) - axis_at - 1))

    gain = one(*shards[0])
    for cut in shards[1:]:
        gain = gain * one(*cut)
    return gain


def centred(rng, shape, scale, most, cuts=(), held_as=jnp.bfloat16):
    gain = block_levels(rng, shape, cuts, -0.22, 0.18) if cuts else 1.0
    result = jax.random.normal(rng, shape, jnp.float32) * scale * gain
    return jnp.minimum(jnp.maximum(result, -most), most).astype(held_as)


def setup_inputs(seed: int = 0) -> dict:
    keys = jax.random.split(jax.random.key(seed), 5)
    return {
        "acts": centred(keys[0], (TOKENS, D), 1.0, 6.0, ((0, 256),)),
        "grads_out": centred(keys[1], (TOKENS, 2 * KVDIM), ((TOK_DEV * N_FSDP) ** -0.5), 0.1875, ((0, 256),)),
        "error": centred(keys[2], (N_REP, 2, D, KVDIM), 1.0, 6.0, ((0, 32), (2, 8))),
        "warm_q": centred(keys[3], (2, RANK, KVDIM), 1.0, 6.0, (), jnp.float32),
    }


def whiten(p_raw):
    gram = jnp.einsum('kra,ksa->krs', p_raw, p_raw, precision=lax.Precision.HIGHEST)
    lower = jnp.linalg.cholesky(gram)
    return lax.linalg.triangular_solve(lower, p_raw, left_side=True, lower=True)

def reference(acts, grads_out, error, warm_q):
    group = TOK_DEV * N_FSDP
    x_all = acts.reshape(N_REP, group, D)
    d_all = grads_out.reshape(N_REP, group, 2 * KVDIM)

    def build(triple):
        x_rep, d_rep, e_rep = triple
        grad = lax.dot_general(x_rep.astype(jnp.float32), d_rep.astype(jnp.float32), (((0,), (0,)), ((), ())), preferred_element_type=jnp.float32)
        grad = grad.reshape(D, 2, KVDIM).transpose(1, 0, 2)
        return grad + e_rep.astype(jnp.float32)
    merged = lax.map(build, (x_all, d_all, error))
    q_now = warm_q
    p_hat = None
    for turn_index in range(POWER):
        p_raw = jnp.einsum('krc,nkac->kra', q_now, merged, precision=lax.Precision.HIGHEST) / N_REP
        p_hat = whiten(p_raw)
        q_now = jnp.einsum('kra,nkac->krc', p_hat, merged, precision=lax.Precision.HIGHEST) / N_REP
    approx = jnp.einsum('kra,krc->kac', p_hat, q_now, precision=lax.Precision.HIGHEST)
    new_error = (merged - approx[None]).astype(jnp.bfloat16)
    return (new_error, p_hat * math.sqrt(D), q_now)
```

```python
import math

import jax
import jax.numpy as jnp
from jax import lax
from jax.sharding import PartitionSpec as P

D = 8192
POWER = 2
BF16 = jnp.bfloat16
F32 = jnp.float32


def halves(x):
    high = lax.reduce_precision(x, 8, 7)
    return high.astype(BF16), (x - high).astype(BF16)


def stacked(x):
    return jnp.concatenate(halves(x), axis=-2)


def folded(x):
    rank = x.shape[-2] // 2
    return x[..., :rank, :] + x[..., rank:, :]


def product(spec, left, right):
    return jnp.einsum(spec, left, right, preferred_element_type=F32)


def fold_columns(x, parts):
    width = x.shape[1] // parts
    return jnp.concatenate([x[:, i * width : (i + 1) * width] for i in range(parts)], 0)


def unfold_columns(x, parts):
    height = x.shape[0] // parts
    return jnp.concatenate([x[i * height : (i + 1) * height] for i in range(parts)], 1)


def swap(x, axis):
    return lax.all_to_all(x, axis, 0, 0, tiled=True)


def total(x, axis):
    n = lax.axis_size(axis)
    mine = swap(x, axis).reshape(n, x.shape[0] // n, x.shape[1]).sum(0)
    everywhere = jnp.broadcast_to(mine[None], (n,) + mine.shape)
    return swap(everywhere.reshape(x.shape), axis)


def on_device(acts, grads_out, error, warm_q):
    err = error[0]
    rank = warm_q.shape[1]
    rows, width = err.shape[1], err.shape[2]
    tokens = acts.shape[0]
    fsdp = lax.axis_size("fsdp")
    replicas = lax.axis_size("rep")
    everyone = replicas * fsdp

    q_halves = stacked(warm_q)
    w = folded(product("krc,tkc->krt", q_halves, grads_out.reshape(tokens, 2, width)))
    w_high, w_low = halves(w.reshape(2 * rank, tokens))
    w_rows = jnp.concatenate(
        [unfold_columns(w_high, 4), unfold_columns(w_low, 4)], axis=1
    )
    extra = w_rows.shape[0]
    blocks = jnp.concatenate(
        [
            acts.reshape(tokens, fsdp, rows).transpose(1, 0, 2),
            jnp.broadcast_to(w_rows[None], (fsdp,) + w_rows.shape),
        ],
        axis=1,
    )
    got = lax.all_to_all(blocks, "fsdp", 0, 0, tiled=True)
    x = got[:, :tokens].reshape(fsdp * tokens, rows)
    w_got = got[:, tokens:].reshape(fsdp, extra, 2, 2, 2, extra * 8)
    w_all = w_got.transpose(3, 2, 4, 1, 0, 5).reshape(2, 2 * rank, fsdp * tokens)

    grads_out, _ = lax.optimization_barrier((grads_out, got))
    d = lax.all_gather(grads_out, "fsdp", axis=0, tiled=True)

    p_part = folded(product("krt,ta->kra", w_all, x)) + folded(
        product("krc,kac->kra", q_halves, err)
    )

    grad = lax.dot_general(x, d, (((0,), (0,)), ((), ())), preferred_element_type=F32)
    merged = grad.reshape(rows, 2, width).transpose(1, 0, 2) + err.astype(F32)
    m_high, m_low = halves(merged)

    def times_merged(spec, left):
        high, low = halves(left)
        both = jnp.concatenate([high, low], axis=-2)
        return folded(product(spec, both, m_high)) + product(spec, high, m_low)

    q_now = None
    for turn in range(POWER):
        if turn:
            p_part = times_merged("krc,kac->kra", q_now)
        p_fold = fold_columns(p_part.reshape(2 * rank, rows), 4)
        p_raw = unfold_columns(total(p_fold, "rep"), 4) / replicas
        p_raw = p_raw.reshape(2, rank, rows)
        gram_part = jnp.einsum(
            "kra,ksa->krs", p_raw, p_raw, precision=lax.Precision.HIGHEST
        )
        q_part = times_merged("kra,kac->krc", p_raw)
        sent = jnp.concatenate(
            [
                fold_columns(q_part.reshape(2 * rank, width), 4),
                fold_columns(gram_part.reshape(2 * rank, rank), 4),
            ],
            axis=1,
        )
        summed = total(sent, ("rep", "fsdp")) / replicas
        q_raw = unfold_columns(summed[:, : width // 4], 4).reshape(2, rank, width)
        gram = unfold_columns(summed[:, width // 4 :], 4).reshape(2, rank, rank)
        lower = jnp.linalg.cholesky(gram)
        q_now = lax.linalg.triangular_solve(lower, q_raw, left_side=True, lower=True)
    p_hat = lax.linalg.triangular_solve(lower, p_raw, left_side=True, lower=True)
    p_halves, q_last = stacked(p_hat), halves(q_now)
    both = jnp.concatenate([q_last[0], q_last[0]], axis=1)
    approx = product("kra,krc->kac", p_halves, both) + product(
        "kra,krc->kac", p_halves[:, :rank], q_last[1]
    )
    new_error = (merged - approx).astype(BF16)[None]
    return (new_error, p_hat * math.sqrt(D), q_now)


def solution(mesh):
    in_specs = (
        P(("rep", "fsdp"), None),
        P(("rep", "fsdp"), None),
        P("rep", None, "fsdp", None),
        P(),
    )
    out_specs = (P("rep", None, "fsdp", None), P(None, None, "fsdp"), P())
    return jax.shard_map(
        on_device, mesh=mesh, in_specs=in_specs, out_specs=out_specs, check_vma=False
    )
```

```python
import functools
import math

import jax
import jax.numpy as jnp
from jax import lax
from jax.experimental import pallas as pl
from jax.experimental.pallas import tpu as pltpu
from jax.sharding import Mesh, PartitionSpec as P

D = 8192
BF16 = jnp.bfloat16
F32 = jnp.float32
REP = ("z", "x")
FSDP = ("y", "core")
VMEM = pl.BlockSpec(memory_space=pltpu.VMEM)
HBM = pl.BlockSpec(memory_space=pltpu.HBM)
MEGA = 1024 * 1024
CUTS = 4


def halves(x):
    high = x.astype(BF16)
    return high, (x - high.astype(F32)).astype(BF16)


def dot(left, right, dims):
    return lax.dot_general(left, right, (dims, ((), ())), preferred_element_type=F32)


def exact(left, right, dims):
    return lax.dot_general(
        left,
        right,
        (dims, ((), ())),
        precision=lax.Precision.HIGHEST,
        preferred_element_type=F32,
    )


def narrow(x, rank):
    return x[:rank] + x[rank : 2 * rank]


def stack(ref, value, row, lane):
    height, width = value.shape[0], value.shape[1] // CUTS
    step = ref.shape[0] // CUTS
    for i in range(CUTS):
        ref[i * step + row : i * step + row + height, lane : lane + width] = value[
            :, i * width : (i + 1) * width
        ]


def unstack(value):
    height = value.shape[0] // CUTS
    return jnp.concatenate(
        [value[i * height : (i + 1) * height] for i in range(CUTS)], axis=1
    )


def prepare(acts, grads_out, warm_q, out, sems):
    parts, height, rows = out.shape
    tokens = acts.shape[0]
    piece = height - tokens
    moves = [
        pltpu.make_async_copy(
            acts.at[:, pl.ds(i * rows, rows)], out.at[i, pl.ds(0, tokens)], sems.at[i]
        )
        for i in range(parts)
    ]
    for move in moves:
        move.start()
    rank, width = warm_q.shape[1:]
    per = rank // piece
    for k in range(2):
        left = jnp.concatenate(halves(warm_q[k]), axis=0)
        grads = grads_out[:, k * width : (k + 1) * width]
        w = narrow(dot(left, grads, ((1,), (1,))), rank)
        for half, value in enumerate(halves(w)):
            for b in range(per):
                at = (half * 2 * per + k * per + b) * tokens
                for i in range(parts):
                    out[i, tokens:height, at : at + tokens] = value[
                        b * piece : (b + 1) * piece
                    ]
    for move in moves:
        move.wait()


def error_part(error, warm_q, out):
    rank = warm_q.shape[1]
    for k in range(2):
        left = jnp.concatenate(halves(warm_q[k]), axis=0)
        out[k * rank : (k + 1) * rank] = narrow(
            dot(left, error[0, k], ((1,), (1,))), rank
        )


def first_left(got, p_error, out, w):
    parts, height, _ = got.shape
    tokens = w.shape[1] // parts
    piece = height - tokens
    total = w.shape[0] // piece
    for s in range(parts):
        for b in range(total):
            w[b * piece : (b + 1) * piece, s * tokens : (s + 1) * tokens] = got[
                s, tokens:height, b * tokens : (b + 1) * tokens
            ]
    p = p_error[...]
    both = jnp.zeros((w.shape[0], got.shape[2]), F32)
    for s in range(0, parts, 2):
        x = jnp.concatenate([got[s, :tokens], got[s + 1, :tokens]], axis=0)
        both += dot(w[:, s * tokens : (s + 2) * tokens], x, ((1,), (0,)))
    stack(out, p + narrow(both, p.shape[0]), 0, 0)


def merge(got, d, error, high, low):
    parts = got.shape[0]
    tokens = d.shape[0] // parts
    x = jnp.concatenate([got[s, :tokens] for s in range(parts)], axis=0)
    for k in range(2):
        width = error.shape[3]
        grad = dot(x, d[:, k * width : (k + 1) * width], ((0,), (0,)))
        high[k], low[k] = halves(grad + error[0, k].astype(F32))


def fetch(high, low, high_here, low_here, sems):
    moves = []
    for k in range(2):
        pair = [
            pltpu.make_async_copy(high.at[k], high_here.at[k], sems.at[2 * k]),
            pltpu.make_async_copy(low.at[k], low_here.at[k], sems.at[2 * k + 1]),
        ]
        for move in pair:
            move.start()
        moves.append(pair)
    return moves


def multiply(left, high, low, dims):
    left_high, left_low = halves(left)
    both = jnp.concatenate([left_high, left_low], axis=0)
    return narrow(dot(both, high, dims), left.shape[0]) + dot(left_high, low, dims)


def right_factor(replicas, rank, p_sum, high, low, p_out, out, high_here, low_here, sems):
    moves = fetch(high, low, high_here, low_here, sems)
    p = unstack(p_sum[...]) / replicas
    p_out[...] = p
    mine = [p[k * rank : (k + 1) * rank] for k in range(2)]
    grams = [exact(x, x, ((1,), (1,))) for x in mine]
    for k in range(2):
        for move in moves[k]:
            move.wait()
        q = multiply(mine[k], high_here[k], low_here[k], ((1,), (0,)))
        stack(out.at[k], q, 0, 0)
        stack(out.at[k], grams[k], 0, q.shape[1] // CUTS)


def inverse_factors(grams):
    n = grams[0].shape[0]
    row = lax.broadcasted_iota(jnp.int32, (n, n), 0)
    column = lax.broadcasted_iota(jnp.int32, (n, n), 1)
    same = row == column
    one = same.astype(F32)
    below = lax.broadcasted_iota(jnp.int32, (n, 2 * n), 0)
    ts = [jnp.concatenate([gram, one], axis=1) for gram in grams]
    for j in range(n - 1):
        for i, t in enumerate(ts):
            pivot_row = t[j : j + 1] / t[j : j + 1, j : j + 1]
            factor = jnp.where(below > j, jnp.broadcast_to(t[:, j : j + 1], t.shape), 0.0)
            ts[i] = t - factor * pivot_row
    inverses = []
    for t in ts:
        pivots = jnp.sum(jnp.where(same, t[:, :n], 0.0), axis=1, keepdims=True)
        inverses.append(t[:, n:] / jnp.sqrt(pivots))
    return inverses


def solved(summed, replicas, rank, width):
    mine = [unstack(summed[k, :, : width // CUTS]) / replicas for k in range(2)]
    last = (width + rank) // CUTS
    inverses = inverse_factors(
        [unstack(summed[k, :, width // CUTS : last]) / replicas for k in range(2)]
    )
    return inverses, [exact(x, y, ((1,), (0,))) for x, y in zip(inverses, mine)]


def left_factor(replicas, rank, q_sum, high, low, out, high_here, low_here, sems):
    moves = fetch(high, low, high_here, low_here, sems)
    _, q = solved(q_sum[...], replicas, rank, high.shape[2])
    for k in range(2):
        for move in moves[k]:
            move.wait()
        p = multiply(q[k], high_here[k], low_here[k], ((1,), (1,)))
        stack(out, p, k * rank, 0)


def finish(
    replicas, rank, q_sum, p_raw, high, low, new_error, p_factor, q_factor, *scratch
):
    high_here, low_here, sems, out, out_sems = scratch
    rows, width = high.shape[1:]
    moves = fetch(high, low, high_here, low_here, sems)
    inverses, q = solved(q_sum[...], replicas, rank, width)
    cut = rows // CUTS
    sends = []
    for k in range(2):
        q_factor[k] = q[k]
        p_hat = exact(inverses[k], p_raw[k * rank : (k + 1) * rank], ((1,), (0,)))
        p_factor[k] = p_hat * math.sqrt(D)
        p_high, p_low = halves(p_hat)
        q_high, q_low = halves(q[k])
        ps = jnp.concatenate([p_high, p_low, p_high, p_low], axis=0)
        qs = jnp.concatenate([q_high, q_high, q_low, q_low], axis=0)
        for move in moves[k]:
            move.wait()
        for i in range(CUTS):
            at = slice(i * cut, (i + 1) * cut)
            approx = dot(ps[:, at], qs, ((0,), (0,)))
            merged = high_here[k, at].astype(F32) + low_here[k, at].astype(F32)
            out[k, at] = (merged - approx).astype(BF16)
            send = pltpu.make_async_copy(
                out.at[k, at], new_error.at[0, k, at], out_sems.at[CUTS * k + i]
            )
            send.start()
            sends.append(send)
    for send in sends:
        send.wait()


def call(kernel, outs, *args, space=52, cost=None, **kw):
    params = pltpu.CompilerParams(vmem_limit_bytes=space * MEGA)
    if cost is not None:
        kw["cost_estimate"] = pl.CostEstimate(
            flops=cost[0], bytes_accessed=cost[1], transcendentals=0
        )
    kw.setdefault("in_specs", [VMEM] * len(args))
    kw.setdefault("out_specs", [VMEM] * len(outs))
    return pl.pallas_call(kernel, out_shape=outs, compiler_params=params, **kw)(*args)


def array(shape, dtype):
    return jax.ShapeDtypeStruct(shape, dtype)


def swap(x, axis):
    return lax.all_to_all(x, axis, 0, 0, tiled=True)


def shared(x, axis):
    n = lax.axis_size(axis)
    return swap(x, axis).reshape(n, x.shape[0] // n, x.shape[1]).sum(0)


def copied(x, axis):
    everywhere = jnp.broadcast_to(x[None], (lax.axis_size(axis),) + x.shape)
    return swap(everywhere.reshape(-1, x.shape[1]), axis)


def total(x, axis):
    return copied(shared(x, axis), axis)


def total_everywhere(x):
    core = lax.axis_index("core")
    flip = [(0, 1), (1, 0)]
    given = lax.dynamic_index_in_dim(x, 1 - core, 0, keepdims=False)
    kept = lax.dynamic_index_in_dim(x, core, 0, keepdims=False)
    mine = shared(kept + lax.ppermute(given, "core", flip), ("x", "y"))
    tall = mine.shape[0]
    mine = copied(mine, "z").reshape(-1, tall, mine.shape[1]).sum(0)
    mine = copied(mine, ("x", "y"))
    other = lax.ppermute(mine, "core", flip)
    first = core == 0
    return jnp.stack([jnp.where(first, mine, other), jnp.where(first, other, mine)])


def on_device(acts, grads_out, error, warm_q):
    _, rank, width = warm_q.shape
    rows = error.shape[2]
    tokens = acts.shape[0]
    fsdp = lax.axis_size(FSDP)
    replicas = lax.axis_size(REP)
    piece = 4 * rank * tokens // rows
    pairs = 2 * rank

    (blocks,) = call(
        prepare,
        [array((fsdp, tokens + piece, rows), BF16)],
        acts,
        grads_out,
        warm_q,
        in_specs=[HBM, VMEM, VMEM],
        scratch_shapes=[pltpu.SemaphoreType.DMA((fsdp,))],
    )
    got = swap(blocks, FSDP)
    (p_error,) = call(error_part, [array((pairs, rows), F32)], error, warm_q, cost=(10**10, 10**8))
    grads_out, _, got = lax.optimization_barrier((grads_out, p_error, got))
    d = lax.all_gather(grads_out, FSDP, axis=0, tiled=True)

    folded = array((CUTS * pairs, rows // CUTS), F32)
    (p_part,) = call(
        first_left,
        [folded],
        got,
        p_error,
        space=16,
        scratch_shapes=[pltpu.VMEM((2 * pairs, fsdp * tokens), BF16)],
    )
    p_sum = total(p_part, REP)
    cut = rows // 4
    high, low = call(
        merge,
        [array((2, rows, width), BF16)] * 2,
        got,
        d,
        error,
        grid=(4,),
        in_specs=[
            pl.BlockSpec((fsdp, tokens + piece, cut), lambda i: (0, 0, i)),
            pl.BlockSpec((fsdp * tokens, 2 * width), lambda i: (0, 0)),
            pl.BlockSpec((1, 2, cut, width), lambda i: (0, 0, i, 0)),
        ],
        out_specs=[pl.BlockSpec((2, cut, width), lambda i: (0, i, 0))] * 2,
    )

    local = [
        pltpu.VMEM((2, rows, width), BF16),
        pltpu.VMEM((2, rows, width), BF16),
        pltpu.SemaphoreType.DMA((4,)),
    ]

    def right(p_sum):
        p_raw, sent = call(
            functools.partial(right_factor, replicas, rank),
            [
                array((pairs, rows), F32),
                array((2, CUTS * rank, (width + rank) // CUTS), F32),
            ],
            p_sum,
            high,
            low,
            in_specs=[VMEM, HBM, HBM],
            scratch_shapes=local,
        )
        return p_raw, total_everywhere(sent)

    _, q_sum = right(p_sum)
    (p_part,) = call(
        functools.partial(left_factor, replicas, rank),
        [folded],
        q_sum,
        high,
        low,
        in_specs=[VMEM, HBM, HBM],
        scratch_shapes=local,
    )
    p_raw, q_sum = right(total(p_part, REP))
    return call(
        functools.partial(finish, replicas, rank),
        [
            array((1, 2, rows, width), BF16),
            array((2, rank, rows), F32),
            array((2, rank, width), F32),
        ],
        q_sum,
        p_raw,
        high,
        low,
        in_specs=[VMEM, VMEM, HBM, HBM],
        out_specs=[HBM, VMEM, VMEM],
        scratch_shapes=local
        + [pltpu.VMEM((2, rows, width), BF16), pltpu.SemaphoreType.DMA((2 * CUTS,))],
    )


def solution(mesh):
    devices = mesh.devices.reshape(8, 4, 4, 2)
    torus = Mesh(devices, REP + FSDP)
    in_specs = (
        P(REP + FSDP, None),
        P(REP + FSDP, None),
        P(REP, None, FSDP, None),
        P(),
    )
    out_specs = (P(REP, None, FSDP, None), P(None, None, FSDP), P())
    return jax.shard_map(
        on_device, mesh=torus, in_specs=in_specs, out_specs=out_specs, check_vma=False
    )
```

```python
import functools
import math

import jax
import jax.numpy as jnp
from jax import lax
from jax.experimental import pallas as pl
from jax.experimental.pallas import tpu as pltpu
from jax.sharding import Mesh, PartitionSpec as P

D = 8192
BF16 = jnp.bfloat16
F32 = jnp.float32
REP = ("z", "x")
FSDP = ("y", "core")
VMEM = pl.BlockSpec(memory_space=pltpu.VMEM)
HBM = pl.BlockSpec(memory_space=pltpu.HBM)
MEGA = 1024 * 1024
CUTS = 4
PIECES = 2


def halves(x):
    high = x.astype(BF16)
    return high, (x - high.astype(F32)).astype(BF16)


def dot(left, right, dims):
    return lax.dot_general(left, right, (dims, ((), ())), preferred_element_type=F32)


def exact(left, right, dims):
    return lax.dot_general(
        left,
        right,
        (dims, ((), ())),
        precision=lax.Precision.HIGHEST,
        preferred_element_type=F32,
    )


def narrow(x, rank):
    return x[:rank] + x[rank : 2 * rank]


def stack(ref, value, row, lane):
    height, width = value.shape[0], value.shape[1] // CUTS
    step = ref.shape[0] // CUTS
    for i in range(CUTS):
        ref[i * step + row : i * step + row + height, lane : lane + width] = value[
            :, i * width : (i + 1) * width
        ]


def unstack(value):
    height = value.shape[0] // CUTS
    return jnp.concatenate(
        [value[i * height : (i + 1) * height] for i in range(CUTS)], axis=1
    )


def prepare(acts, grads_out, warm_q, out, here, w_rows, in_sems, out_sems):
    parts, height, rows = out.shape
    tokens = acts.shape[0]
    piece = height - tokens
    moves = [
        pltpu.make_async_copy(
            acts.at[:, pl.ds(i * rows, rows)], here.at[i], in_sems.at[i]
        )
        for i in range(parts)
    ]
    for move in moves:
        move.start()
    sends = []
    for i in range(parts):
        moves[i].wait()
        sends.append(
            pltpu.make_async_copy(
                here.at[i], out.at[i, pl.ds(0, tokens)], out_sems.at[i]
            )
        )
        sends[-1].start()
    rank, width = warm_q.shape[1:]
    per = rank // piece
    for k in range(2):
        left = jnp.concatenate(halves(warm_q[k]), axis=0)
        grads = grads_out[:, k * width : (k + 1) * width]
        w = narrow(dot(left, grads, ((1,), (1,))), rank)
        for half, value in enumerate(halves(w)):
            for b in range(per):
                at = (half * 2 * per + k * per + b) * tokens
                w_rows[:, at : at + tokens] = value[b * piece : (b + 1) * piece]
    for i in range(parts):
        sends.append(
            pltpu.make_async_copy(
                w_rows, out.at[i, pl.ds(tokens, piece)], out_sems.at[parts + i]
            )
        )
        sends[-1].start()
    for send in sends:
        send.wait()


def error_part(error, warm_q, out):
    rank = warm_q.shape[1]
    for k in range(2):
        left = jnp.concatenate(halves(warm_q[k]), axis=0)
        out[k * rank : (k + 1) * rank] = narrow(
            dot(left, error[0, k], ((1,), (1,))), rank
        )


def first_left(got, p_error, out, w):
    parts, height, _ = got.shape
    tokens = w.shape[1] // parts
    piece = height - tokens
    total = w.shape[0] // piece
    for s in range(parts):
        for b in range(total):
            w[b * piece : (b + 1) * piece, s * tokens : (s + 1) * tokens] = got[
                s, tokens:height, b * tokens : (b + 1) * tokens
            ]
    p = p_error[...]
    both = jnp.zeros((w.shape[0], got.shape[2]), F32)
    for s in range(0, parts, 2):
        x = jnp.concatenate([got[s, :tokens], got[s + 1, :tokens]], axis=0)
        both += dot(w[:, s * tokens : (s + 2) * tokens], x, ((1,), (0,)))
    stack(out, p + narrow(both, p.shape[0]), 0, 0)


def merge(place, got, error, *refs):
    blocks, (high, low), scratch = refs[:8], refs[8:10], refs[10:]
    x, d, e, high_here, low_here, in_sems, error_sems, out_sems = scratch
    y, core = place[0], place[1]
    tokens = d.shape[0] // 8
    rows, width = e.shape[1:]
    cut = rows // CUTS
    moves = []
    for i in range(8):
        step, other = divmod(i, 2)
        source = 2 * lax.rem(y + 4 - step, 4) + (1 - core if other else core)
        at = pl.ds(i * tokens, tokens)
        moves += [
            pltpu.make_async_copy(blocks[i], d.at[at], in_sems.at[i]),
            pltpu.make_async_copy(
                got.at[source, pl.ds(0, tokens)], x.at[at], in_sems.at[8 + i]
            ),
        ]
    errors = [
        pltpu.make_async_copy(
            error.at[0, :, pl.ds(i * cut, cut)],
            e.at[:, pl.ds(i * cut, cut)],
            error_sems.at[i],
        )
        for i in range(CUTS)
    ]
    for move in moves + errors:
        move.start()
    for move in moves:
        move.wait()
    sends = []
    for i in range(CUTS):
        at = slice(i * cut, (i + 1) * cut)
        errors[i].wait()
        for k in range(2):
            grad = dot(x[:, at], d[:, k * width : (k + 1) * width], ((0,), (0,)))
            merged_high, merged_low = halves(grad + e[k, at].astype(F32))
            high_here[k, at] = merged_high
            low_here[k, at] = merged_low
            for here, there, n in ((high_here, high, 0), (low_here, low, 1)):
                send = pltpu.make_async_copy(
                    here.at[k, at], there.at[k, at], out_sems.at[4 * i + 2 * k + n]
                )
                send.start()
                sends.append(send)
    for send in sends:
        send.wait()


def fetch(high, low, high_here, low_here, sems):
    cut = high.shape[1] // PIECES
    moves = []
    for k in range(2):
        for i in range(PIECES):
            at = pl.ds(i * cut, cut)
            n = 2 * (PIECES * k + i)
            moves.append(
                [
                    pltpu.make_async_copy(
                        high.at[k, at], high_here.at[k, at], sems.at[n]
                    ),
                    pltpu.make_async_copy(
                        low.at[k, at], low_here.at[k, at], sems.at[n + 1]
                    ),
                ]
            )
    for pair in moves:
        for move in pair:
            move.start()
    return moves


def multiply(left, high, low, dims):
    left_high, left_low = halves(left)
    both = jnp.concatenate([left_high, left_low], axis=0)
    return narrow(dot(both, high, dims), left.shape[0]) + dot(left_high, low, dims)


def right_factor(replicas, rank, p_sum, high, low, p_out, out, high_here, low_here, sems):
    moves = fetch(high, low, high_here, low_here, sems)
    p = unstack(p_sum[...]) / replicas
    p_out[...] = p
    mine = [p[k * rank : (k + 1) * rank] for k in range(2)]
    grams = [exact(x, x, ((1,), (1,))) for x in mine]
    for k in range(2):
        for pair in moves[PIECES * k : PIECES * (k + 1)]:
            for move in pair:
                move.wait()
        q = multiply(mine[k], high_here[k], low_here[k], ((1,), (0,)))
        stack(out.at[k], q, 0, 0)
        stack(out.at[k], grams[k], 0, q.shape[1] // CUTS)


def inverse_factors(grams):
    n = grams[0].shape[0]
    row = lax.broadcasted_iota(jnp.int32, (n, n), 0)
    column = lax.broadcasted_iota(jnp.int32, (n, n), 1)
    same = row == column
    one = same.astype(F32)
    below = lax.broadcasted_iota(jnp.int32, (n, 2 * n), 0)
    ts = [jnp.concatenate([gram, one], axis=1) for gram in grams]
    for j in range(n - 1):
        for i, t in enumerate(ts):
            pivot_row = t[j : j + 1] / t[j : j + 1, j : j + 1]
            factor = jnp.broadcast_to(t[:, j : j + 1], t.shape)
            ts[i] = t - jnp.where(below > j, factor, 0.0) * pivot_row
    inverses = []
    for t in ts:
        pivots = jnp.sum(jnp.where(same, t[:, :n], 0.0), axis=1, keepdims=True)
        inverses.append(t[:, n:] / jnp.sqrt(pivots))
    return inverses


def summed_factors(summed, replicas, rank, width):
    last = (width + rank) // CUTS
    q = [unstack(summed[k, :, : width // CUTS]) / replicas for k in range(2)]
    grams = [unstack(summed[k, :, width // CUTS : last]) / replicas for k in range(2)]
    return q, inverse_factors(grams)


def left_factor(replicas, rank, q_sum, high, low, out, high_here, low_here, sems):
    moves = fetch(high, low, high_here, low_here, sems)
    q, inverses = summed_factors(q_sum[...], replicas, rank, high.shape[2])
    cut = high.shape[1] // PIECES
    p = []
    for n in range(2 * PIECES):
        for move in moves[n]:
            move.wait()
        k, i = divmod(n, PIECES)
        at = slice(i * cut, (i + 1) * cut)
        p.append(multiply(q[k], high_here[k, at], low_here[k, at], ((1,), (1,))))
    for k in range(2):
        mine = jnp.concatenate(p[PIECES * k : PIECES * (k + 1)], axis=1)
        stack(out, exact(inverses[k], mine, ((1,), (0,))), k * rank, 0)


def finish(
    replicas, rank, q_sum, p_raw, high, low, new_error, p_factor, q_factor, *scratch
):
    high_here, low_here, sems, out, out_sems = scratch
    rows, width = high.shape[1:]
    moves = fetch(high, low, high_here, low_here, sems)
    q_raw, inverses = summed_factors(q_sum[...], replicas, rank, width)
    cut = rows // CUTS
    sends = []
    for k in range(2):
        q = exact(inverses[k], q_raw[k], ((1,), (0,)))
        q_factor[k] = q
        p_hat = exact(inverses[k], p_raw[k * rank : (k + 1) * rank], ((1,), (0,)))
        p_factor[k] = p_hat * math.sqrt(D)
        p_high, p_low = halves(p_hat)
        q_high, q_low = halves(q)
        ps = jnp.concatenate([p_high, p_low, p_high, p_low], axis=0)
        qs = jnp.concatenate([q_high, q_high, q_low, q_low], axis=0)
        for i in range(CUTS):
            if i % (CUTS // PIECES) == 0:
                for move in moves[PIECES * k + i * PIECES // CUTS]:
                    move.wait()
            at = slice(i * cut, (i + 1) * cut)
            approx = dot(ps[:, at], qs, ((0,), (0,)))
            merged = high_here[k, at].astype(F32) + low_here[k, at].astype(F32)
            out[k, at] = (merged - approx).astype(BF16)
            send = pltpu.make_async_copy(
                out.at[k, at], new_error.at[0, k, at], out_sems.at[CUTS * k + i]
            )
            send.start()
            sends.append(send)
    for send in sends:
        send.wait()


def call(kernel, outs, *args, space=52, cost=None, **kw):
    params = pltpu.CompilerParams(vmem_limit_bytes=space * MEGA)
    if cost is not None:
        kw["cost_estimate"] = pl.CostEstimate(
            flops=cost[0], bytes_accessed=cost[1], transcendentals=0
        )
    kw.setdefault("in_specs", [VMEM] * len(args))
    kw.setdefault("out_specs", [VMEM] * len(outs))
    return pl.pallas_call(kernel, out_shape=outs, compiler_params=params, **kw)(*args)


def array(shape, dtype):
    return jax.ShapeDtypeStruct(shape, dtype)


def swap(x, axis):
    return lax.all_to_all(x, axis, 0, 0, tiled=True)


def shared(x, axis):
    n = lax.axis_size(axis)
    return swap(x, axis).reshape(n, x.shape[0] // n, x.shape[1]).sum(0)


def copied(x, axis):
    everywhere = jnp.broadcast_to(x[None], (lax.axis_size(axis),) + x.shape)
    return swap(everywhere.reshape(-1, x.shape[1]), axis)


def total(x, axis):
    return copied(shared(x, axis), axis)


def total_everywhere(x):
    core = lax.axis_index("core")
    flip = [(0, 1), (1, 0)]
    given = lax.dynamic_index_in_dim(x, 1 - core, 0, keepdims=False)
    kept = lax.dynamic_index_in_dim(x, core, 0, keepdims=False)
    mine = shared(kept + lax.ppermute(given, "core", flip), ("x", "y"))
    tall = mine.shape[0]
    mine = copied(mine, "z").reshape(-1, tall, mine.shape[1]).sum(0)
    mine = copied(mine, ("x", "y"))
    other = lax.ppermute(mine, "core", flip)
    first = core == 0
    return jnp.stack([jnp.where(first, mine, other), jnp.where(first, other, mine)])


def on_device(acts, grads_out, error, warm_q):
    _, rank, width = warm_q.shape
    rows = error.shape[2]
    tokens = acts.shape[0]
    fsdp = lax.axis_size(FSDP)
    replicas = lax.axis_size(REP)
    piece = 4 * rank * tokens // rows
    pairs = 2 * rank

    (blocks,) = call(
        prepare,
        [array((fsdp, tokens + piece, rows), BF16)],
        acts,
        grads_out,
        warm_q,
        space=60,
        in_specs=[HBM, VMEM, VMEM],
        out_specs=[HBM],
        scratch_shapes=[
            pltpu.VMEM((fsdp, tokens, rows), BF16),
            pltpu.VMEM((piece, rows), BF16),
            pltpu.SemaphoreType.DMA((fsdp,)),
            pltpu.SemaphoreType.DMA((2 * fsdp,)),
        ],
    )
    got = swap(blocks, FSDP)
    (p_error,) = call(error_part, [array((pairs, rows), F32)], error, warm_q, cost=(10**10, 10**8))
    grads_out, _, got = lax.optimization_barrier((grads_out, p_error, got))
    place = jnp.stack([lax.axis_index("y"), lax.axis_index("core")]).astype(jnp.int32)
    here = [grads_out] + [
        lax.ppermute(grads_out, "y", [(i, (i + step) % 4) for i in range(4)])
        for step in (1, 3, 2)
    ]
    folded = array((CUTS * pairs, rows // CUTS), F32)
    (p_part,) = call(
        first_left,
        [folded],
        got,
        p_error,
        space=16,
        scratch_shapes=[pltpu.VMEM((2 * pairs, fsdp * tokens), BF16)],
    )
    p_mine = shared(p_part, REP)
    *here, _ = lax.optimization_barrier((*here, p_mine))
    here = [here[0], here[1], here[3], here[2]]
    there = [lax.ppermute(block, "core", [(0, 1), (1, 0)]) for block in here]
    d = [block for pair in zip(here, there) for block in pair]
    p_sum = copied(p_mine, REP)
    halved = array((2, rows, width), BF16)
    folded_q = array((2, CUTS * rank, (width + rank) // CUTS), F32)
    high, low = call(
        merge,
        [halved, halved],
        place,
        got,
        error,
        *d,
        in_specs=[pl.BlockSpec(memory_space=pltpu.SMEM)] + [HBM] * 10,
        out_specs=[HBM, HBM],
        scratch_shapes=[
            pltpu.VMEM((fsdp * tokens, rows), BF16),
            pltpu.VMEM((fsdp * tokens, 2 * width), BF16),
            pltpu.VMEM((2, rows, width), BF16),
            pltpu.VMEM((2, rows, width), BF16),
            pltpu.VMEM((2, rows, width), BF16),
            pltpu.SemaphoreType.DMA((16,)),
            pltpu.SemaphoreType.DMA((CUTS,)),
            pltpu.SemaphoreType.DMA((4 * CUTS,)),
        ],
    )
    local = [
        pltpu.VMEM((2, rows, width), BF16),
        pltpu.VMEM((2, rows, width), BF16),
        pltpu.SemaphoreType.DMA((4 * PIECES,)),
    ]

    def right(p_sum):
        p_raw, sent = call(
            functools.partial(right_factor, replicas, rank),
            [array((pairs, rows), F32), folded_q],
            p_sum,
            high,
            low,
            in_specs=[VMEM, HBM, HBM],
            scratch_shapes=local,
        )
        return p_raw, total_everywhere(sent)

    _, q_sum = right(p_sum)
    (p_part,) = call(
        functools.partial(left_factor, replicas, rank),
        [folded],
        q_sum,
        high,
        low,
        in_specs=[VMEM, HBM, HBM],
        scratch_shapes=local,
    )
    p_raw, q_sum = right(total(p_part, REP))
    return call(
        functools.partial(finish, replicas, rank),
        [
            array((1, 2, rows, width), BF16),
            array((2, rank, rows), F32),
            array((2, rank, width), F32),
        ],
        q_sum,
        p_raw,
        high,
        low,
        in_specs=[VMEM, VMEM, HBM, HBM],
        out_specs=[HBM, VMEM, VMEM],
        scratch_shapes=local
        + [pltpu.VMEM((2, rows, width), BF16), pltpu.SemaphoreType.DMA((2 * CUTS,))],
    )


def solution(mesh):
    devices = mesh.devices.reshape(8, 4, 4, 2)
    torus = Mesh(devices, REP + FSDP)
    in_specs = (
        P(REP + FSDP, None),
        P(REP + FSDP, None),
        P(REP, None, FSDP, None),
        P(),
    )
    out_specs = (P(REP, None, FSDP, None), P(None, None, FSDP), P())
    return jax.shard_map(
        on_device, mesh=torus, in_specs=in_specs, out_specs=out_specs, check_vma=False
    )
```

```python
import functools
import math

import jax
import jax.numpy as jnp
from jax import lax
from jax.experimental import pallas as pl
from jax.experimental.pallas import tpu as pltpu
from jax.sharding import Mesh, PartitionSpec as P

D = 8192
BF16 = jnp.bfloat16
F32 = jnp.float32
REP = ("z", "x")
FSDP = ("y", "core")
VMEM = pl.BlockSpec(memory_space=pltpu.VMEM)
HBM = pl.BlockSpec(memory_space=pltpu.HBM)
MEGA = 1024 * 1024
CUTS = 4
PIECES = 2
LANES = 128


def halves(x):
    high = x.astype(BF16)
    return high, (x - high.astype(F32)).astype(BF16)


def dot(left, right, dims):
    return lax.dot_general(left, right, (dims, ((), ())), preferred_element_type=F32)


def exact(left, right, dims):
    return lax.dot_general(
        left,
        right,
        (dims, ((), ())),
        precision=lax.Precision.HIGHEST,
        preferred_element_type=F32,
    )


def narrow(x, rank):
    return x[:rank] + x[rank : 2 * rank]


def stack(ref, value, lane):
    height, width = value.shape[0], value.shape[1] // CUTS
    for i in range(CUTS):
        ref[i * height : (i + 1) * height, lane : lane + width] = value[
            :, i * width : (i + 1) * width
        ]


def unstack(value):
    height = value.shape[0] // CUTS
    return jnp.concatenate(
        [value[i * height : (i + 1) * height] for i in range(CUTS)], axis=1
    )


def pack(ref, pair):
    for h, value in enumerate(pair):
        height = value.shape[0]
        for i in range(value.shape[1] // LANES):
            ref[i * height : (i + 1) * height, h * LANES : (h + 1) * LANES] = value[
                :, i * LANES : (i + 1) * LANES
            ]


def unpack(value, height):
    return [
        jnp.concatenate(
            [
                value[i : i + height, h * LANES : (h + 1) * LANES]
                for i in range(0, value.shape[0], height)
            ],
            axis=1,
        )
        for h in range(2)
    ]


def prepare(acts, grads_out, warm_q, out, here, w_rows, in_sems, out_sems):
    parts, height, rows = out.shape
    tokens = acts.shape[0]
    piece = height - tokens
    moves = [
        pltpu.make_async_copy(
            acts.at[:, pl.ds(i * rows, rows)], here.at[i], in_sems.at[i]
        )
        for i in range(parts)
    ]
    for move in moves:
        move.start()
    sends = []
    for i in range(parts):
        moves[i].wait()
        sends.append(
            pltpu.make_async_copy(
                here.at[i], out.at[i, pl.ds(0, tokens)], out_sems.at[i]
            )
        )
        sends[-1].start()
    rank, width = warm_q.shape[1:]
    per = rank // piece
    for k in range(2):
        left = jnp.concatenate(halves(warm_q[k]), axis=0)
        grads = grads_out[:, k * width : (k + 1) * width]
        w = narrow(dot(left, grads, ((1,), (1,))), rank)
        for half, value in enumerate(halves(w)):
            for b in range(per):
                at = (half * 2 * per + k * per + b) * tokens
                w_rows[:, at : at + tokens] = value[b * piece : (b + 1) * piece]
    for i in range(parts):
        sends.append(
            pltpu.make_async_copy(
                w_rows, out.at[i, pl.ds(tokens, piece)], out_sems.at[parts + i]
            )
        )
        sends[-1].start()
    for send in sends:
        send.wait()


def error_part(place, error, warm_q, out, given):
    given[...] = error[0, 1 - place[1]]
    rank = warm_q.shape[1]
    for k in range(2):
        left = jnp.concatenate(halves(warm_q[k]), axis=0)
        out[k * rank : (k + 1) * rank] = narrow(
            dot(left, error[0, k], ((1,), (1,))), rank
        )


def first_left(got, p_error, out, w):
    parts, height, _ = got.shape
    tokens = w.shape[1] // parts
    piece = height - tokens
    total = w.shape[0] // piece
    for s in range(parts):
        for b in range(total):
            w[b * piece : (b + 1) * piece, s * tokens : (s + 1) * tokens] = got[
                s, tokens:height, b * tokens : (b + 1) * tokens
            ]
    p = p_error[...]
    both = jnp.zeros((w.shape[0], got.shape[2]), F32)
    for s in range(0, parts, 2):
        x = jnp.concatenate([got[s, :tokens], got[s + 1, :tokens]], axis=0)
        both += dot(w[:, s * tokens : (s + 2) * tokens], x, ((1,), (0,)))
    p += narrow(both, p.shape[0])
    rank = p.shape[0] // 2
    pack(out, (p[:rank], p[rank:]))


def merge(place, got, got_other, error, error_other, *refs):
    blocks, outs, scratch = refs[:5], refs[5:9], refs[9:]
    x, d, e, high, low, d_sems, x_sems, e_sems, out_sems = scratch
    y, core = place[0], place[1]
    rows = e.shape[1]
    tokens = blocks[0].shape[0] // 2
    cut = rows // CUTS
    d_moves, at = [], 0
    for i, block in enumerate(blocks):
        tall = block.shape[0]
        d_moves.append(
            pltpu.make_async_copy(block, d.at[pl.ds(at, tall)], d_sems.at[i])
        )
        at += tall
    x_moves, e_moves = [], []
    for h, source in enumerate((got, got_other)):
        for s in range(4):
            first = 2 * lax.rem(y + 4 - s, 4)
            for n, at in ((0, first + core), (1, first + 1 - core)):
                i = 2 * s + n
                x_moves.append(
                    pltpu.make_async_copy(
                        source.at[at, pl.ds(0, tokens)],
                        x.at[h, pl.ds(i * tokens, tokens)],
                        x_sems.at[8 * h + i],
                    )
                )
        for i in range(CUTS):
            at = pl.ds(i * cut, cut)
            part = error_other.at[at] if h else error.at[0, core, at]
            e_moves.append(
                pltpu.make_async_copy(part, e.at[h, at], e_sems.at[CUTS * h + i])
            )
    for move in (
        d_moves + x_moves[:8] + e_moves[:CUTS] + x_moves[8:] + e_moves[CUTS:]
    ):
        move.start()
    for move in d_moves:
        move.wait()
    sends = []
    for h in range(2):
        for move in x_moves[8 * h : 8 * h + 8]:
            move.wait()
        for i in range(CUTS):
            n = CUTS * h + i
            at = slice(i * cut, (i + 1) * cut)
            e_moves[n].wait()
            grad = dot(x[h, :, at], d[...], ((0,), (0,)))
            high[h, at], low[h, at] = halves(grad + e[h, at].astype(F32))
            for m, here in enumerate((high, low)):
                send = pltpu.make_async_copy(
                    here.at[h, at], outs[2 * h + m].at[at], out_sems.at[2 * n + m]
                )
                send.start()
                sends.append(send)
    for send in sends:
        send.wait()


def fetch(sources, high, low, sems):
    cut = high.shape[1] // PIECES
    moves = []
    for h in range(2):
        for i in range(PIECES):
            at = pl.ds(i * cut, cut)
            n = 2 * (PIECES * h + i)
            moves.append(
                [
                    pltpu.make_async_copy(
                        sources[2 * h].at[at], high.at[h, at], sems.at[n]
                    ),
                    pltpu.make_async_copy(
                        sources[2 * h + 1].at[at], low.at[h, at], sems.at[n + 1]
                    ),
                ]
            )
    for both in moves:
        for move in both:
            move.start()
    return moves


def multiply(left, high, low, dims):
    left_high, left_low = halves(left)
    both = jnp.concatenate([left_high, left_low], axis=0)
    return narrow(dot(both, high, dims), left.shape[0]) + dot(left_high, low, dims)


def right_factor(replicas, p_sum, *refs):
    sources, (p_mine, p_given, out, high, low, sems) = refs[:4], refs[4:]
    moves = fetch(sources, high, low, sems)
    p = [x / replicas for x in unpack(p_sum[...], p_mine.shape[0])]
    p_mine[...] = p[0]
    stack(p_given, p[1], 0)
    gram = q = 0.0
    for h in range(2):
        gram += exact(p[h], p[h], ((1,), (1,)))
    for h in range(2):
        for both in moves[PIECES * h : PIECES * (h + 1)]:
            for move in both:
                move.wait()
        q += multiply(p[h], high[h], low[h], ((1,), (0,)))
    stack(out, q, 0)
    stack(out, gram, q.shape[1] // CUTS)


def inverse_factors(grams):
    n = grams[0].shape[0]
    row = lax.broadcasted_iota(jnp.int32, (n, n), 0)
    column = lax.broadcasted_iota(jnp.int32, (n, n), 1)
    same = row == column
    one = same.astype(F32)
    below = lax.broadcasted_iota(jnp.int32, (n, 2 * n), 0)
    ts = [jnp.concatenate([gram, one], axis=1) for gram in grams]
    for j in range(n - 1):
        for i, t in enumerate(ts):
            pivot_row = t[j : j + 1] / t[j : j + 1, j : j + 1]
            factor = jnp.broadcast_to(t[:, j : j + 1], t.shape)
            ts[i] = t - jnp.where(below > j, factor, 0.0) * pivot_row
    inverses = []
    for t in ts:
        pivots = jnp.sum(jnp.where(same, t[:, :n], 0.0), axis=1, keepdims=True)
        inverses.append(t[:, n:] / jnp.sqrt(pivots))
    return inverses


def summed(sums, replicas, rank, width):
    last = (width + rank) // CUTS
    return (
        unstack(sums[:, : width // CUTS]) / replicas,
        unstack(sums[:, width // CUTS : last]) / replicas,
    )


def left_factor(replicas, rank, q_sum, *refs):
    sources, (out, high, low, sems) = refs[:4], refs[4:]
    moves = fetch(sources, high, low, sems)
    q, gram = summed(q_sum[...], replicas, rank, high.shape[2])
    (inverse,) = inverse_factors([gram])
    cut = high.shape[1] // PIECES
    p = []
    for n in range(2 * PIECES):
        for move in moves[n]:
            move.wait()
        h, i = divmod(n, PIECES)
        at = slice(i * cut, (i + 1) * cut)
        p.append(multiply(q, high[h, at], low[h, at], ((1,), (1,))))
    pair = [
        jnp.concatenate(p[PIECES * h : PIECES * (h + 1)], axis=1) for h in range(2)
    ]
    pack(out, [exact(inverse, x, ((1,), (0,))) for x in pair])


def finish(replicas, rank, place, q_mine, other, p_mine, *refs):
    sources, (new_error, p_factor, q_factor), scratch = refs[:4], refs[4:7], refs[7:]
    high, low, sems, out, out_sems, lefts, rights = scratch
    rows, width = high.shape[1:]
    moves = fetch(sources, high, low, sems)
    core = place[1]
    cut = rows // CUTS

    @pl.when(core >= 0)
    def _():
        sums = [
            summed(x, replicas, rank, width) for x in (q_mine[...], other[:, cut:])
        ]
        p_raws = (p_mine[...], unstack(other[:, :cut]))
        inverses = inverse_factors([gram for _, gram in sums])
        for n, p_raw in enumerate(p_raws):
            k = 1 - core if n else core
            q = exact(inverses[n], sums[n][0], ((1,), (0,)))
            q_factor[k] = q
            p_hat = exact(inverses[n], p_raw, ((1,), (0,)))
            p_factor[k] = p_hat * math.sqrt(D)
            p_high, p_low = halves(p_hat)
            q_high, q_low = halves(q)
            lefts[n] = jnp.concatenate([p_high, p_low, p_high, p_low], axis=0)
            rights[n] = jnp.concatenate([q_high, q_high, q_low, q_low], axis=0)
    sends = []
    for n in range(2):
        k = 1 - core if n else core
        for i in range(CUTS):
            if i % (CUTS // PIECES) == 0:
                for move in moves[PIECES * n + i * PIECES // CUTS]:
                    move.wait()
            at = slice(i * cut, (i + 1) * cut)
            approx = dot(lefts[n, :, at], rights[n], ((0,), (0,)))
            merged = high[n, at].astype(F32) + low[n, at].astype(F32)
            out[n, at] = (merged - approx).astype(BF16)
            send = pltpu.make_async_copy(
                out.at[n, at],
                new_error.at[0, k, pl.ds(i * cut, cut)],
                out_sems.at[CUTS * n + i],
            )
            send.start()
            sends.append(send)
    for send in sends:
        send.wait()


def call(kernel, outs, *args, space=52, cost=None, **kw):
    params = pltpu.CompilerParams(vmem_limit_bytes=space * MEGA)
    if cost is not None:
        kw["cost_estimate"] = pl.CostEstimate(
            flops=cost[0], bytes_accessed=cost[1], transcendentals=0
        )
    kw.setdefault("in_specs", [VMEM] * len(args))
    kw.setdefault("out_specs", [VMEM] * len(outs))
    return pl.pallas_call(kernel, out_shape=outs, compiler_params=params, **kw)(*args)


def array(shape, dtype):
    return jax.ShapeDtypeStruct(shape, dtype)


def swap(x, axis):
    return lax.all_to_all(x, axis, 0, 0, tiled=True)


def shared(x, axis):
    n = lax.axis_size(axis)
    return swap(x, axis).reshape(n, x.shape[0] // n, x.shape[1]).sum(0)


def copied(x, axis):
    everywhere = jnp.broadcast_to(x[None], (lax.axis_size(axis),) + x.shape)
    return swap(everywhere.reshape(-1, x.shape[1]), axis)


def total(x, axis):
    return copied(shared(x, axis), axis)


def total_everywhere(x):
    mine = shared(x, ("x", "y"))
    tall = mine.shape[0]
    mine = copied(mine, "z").reshape(-1, tall, mine.shape[1]).sum(0)
    return copied(mine, ("x", "y"))


def flip(x):
    return lax.ppermute(x, "core", [(0, 1), (1, 0)])


def on_device(acts, grads_out, error, warm_q):
    _, rank, width = warm_q.shape
    rows = error.shape[2]
    tokens = acts.shape[0]
    fsdp = lax.axis_size(FSDP)
    replicas = lax.axis_size(REP)
    piece = 4 * rank * tokens // rows
    pairs = 2 * rank

    (blocks,) = call(
        prepare,
        [array((fsdp, tokens + piece, rows), BF16)],
        acts,
        grads_out,
        warm_q,
        space=60,
        in_specs=[HBM, VMEM, VMEM],
        out_specs=[HBM],
        scratch_shapes=[
            pltpu.VMEM((fsdp, tokens, rows), BF16),
            pltpu.VMEM((piece, rows), BF16),
            pltpu.SemaphoreType.DMA((fsdp,)),
            pltpu.SemaphoreType.DMA((2 * fsdp,)),
        ],
    )
    got = swap(blocks, FSDP)

    core = lax.axis_index("core")
    place = jnp.stack([lax.axis_index("y"), core]).astype(jnp.int32)
    late_d, late_error, late_q, _ = lax.optimization_barrier(
        (grads_out, error, warm_q, blocks)
    )
    smem = pl.BlockSpec(memory_space=pltpu.SMEM)
    p_error, error_given = call(
        error_part,
        [array((pairs, rows), F32), array((rows, width), BF16)],
        place,
        late_error,
        late_q,
        in_specs=[smem, VMEM, VMEM],
        cost=(10**10, 10**8),
    )
    d_kept = lax.dynamic_slice_in_dim(late_d, core * width, width, 1)
    d_given = lax.dynamic_slice_in_dim(late_d, (1 - core) * width, width, 1)
    d_here = jnp.concatenate([d_kept, flip(d_given)], axis=0)
    d_here, p_error, got = lax.optimization_barrier((d_here, p_error, got))
    error_other = flip(error_given)

    up = [(i, (i + 1) % 4) for i in range(4)]
    down = [(i, (i + 3) % 4) for i in range(4)]
    d_up, d_down = lax.ppermute(d_here, "y", up), lax.ppermute(d_here, "y", down)
    got_other = flip(got)
    packed = array((rows // LANES * rank, 2 * LANES), F32)
    (p_part,) = call(
        first_left,
        [packed],
        got,
        p_error,
        space=16,
        scratch_shapes=[pltpu.VMEM((2 * pairs, fsdp * tokens), BF16)],
    )
    p_both = shared(p_part, REP)
    first, second = p_both[:, :LANES], p_both[:, LANES:]
    kept = jnp.where(core == 0, first, second)
    given = jnp.where(core == 0, second, first)
    p_piece, _, _ = lax.optimization_barrier(
        (jnp.concatenate([kept, flip(given)], axis=1), d_up, d_down)
    )
    far = [
        lax.ppermute(d_up[:tokens], "y", up),
        lax.ppermute(d_down[tokens:], "y", down),
    ]
    d = [d_here, d_up, *far, d_down]
    p_sum = copied(p_piece, REP)

    part = array((rows, width), BF16)
    local = [
        pltpu.VMEM((2, rows, width), BF16),
        pltpu.VMEM((2, rows, width), BF16),
        pltpu.SemaphoreType.DMA((4 * PIECES,)),
    ]
    merged = call(
        merge,
        [part] * 4,
        place,
        got,
        got_other,
        error,
        error_other,
        *d,
        in_specs=[smem] + [HBM] * 9,
        cost=(4*10**10, 2 * 10**7),
        out_specs=[HBM] * 4,
        scratch_shapes=[
            pltpu.VMEM((2, fsdp * tokens, rows), BF16),
            pltpu.VMEM((fsdp * tokens, width), BF16),
            pltpu.VMEM((2, rows, width), BF16),
            pltpu.VMEM((2, rows, width), BF16),
            pltpu.VMEM((2, rows, width), BF16),
            pltpu.SemaphoreType.DMA((5,)),
            pltpu.SemaphoreType.DMA((16,)),
            pltpu.SemaphoreType.DMA((2 * CUTS,)),
            pltpu.SemaphoreType.DMA((4 * CUTS,)),
        ],
    )
    high, low, high_given, low_given = merged

    def right(p_sum):
        *p_raw, sent = call(
            functools.partial(right_factor, replicas),
            [
                array((rank, rows), F32),
                array((CUTS * rank, rows // CUTS), F32),
                array((CUTS * rank, (width + rank) // CUTS), F32),
            ],
            p_sum,
            *merged,
            in_specs=[VMEM] + [HBM] * 4,
            scratch_shapes=local,
        )
        return p_raw, total_everywhere(sent)

    _, q_sum = right(p_sum)
    (p_part,) = call(
        functools.partial(left_factor, replicas, rank),
        [packed],
        q_sum,
        *merged,
        in_specs=[VMEM] + [HBM] * 4,
        scratch_shapes=local,
    )
    (p_mine, p_given), q_sum = right(total(p_part, REP))
    return call(
        functools.partial(finish, replicas, rank),
        [
            array((1, 2, rows, width), BF16),
            array((2, rank, rows), F32),
            array((2, rank, width), F32),
        ],
        place,
        q_sum,
        flip(jnp.concatenate([p_given, q_sum], axis=1)),
        p_mine,
        high,
        low,
        flip(high_given),
        flip(low_given),
        in_specs=[smem] + [VMEM] * 3 + [HBM] * 4,
        out_specs=[HBM, VMEM, VMEM],
        scratch_shapes=local
        + [
            pltpu.VMEM((2, rows, width), BF16),
            pltpu.SemaphoreType.DMA((2 * CUTS,)),
            pltpu.VMEM((2, 4 * rank, rows), BF16),
            pltpu.VMEM((2, 4 * rank, width), BF16),
        ],
    )


def solution(mesh):
    devices = mesh.devices.reshape(8, 4, 4, 2)
    torus = Mesh(devices, REP + FSDP)
    in_specs = (
        P(REP + FSDP, None),
        P(REP + FSDP, None),
        P(REP, None, FSDP, None),
        P(),
    )
    out_specs = (P(REP, None, FSDP, None), P(None, None, FSDP), P())
    return jax.shard_map(
        on_device, mesh=torus, in_specs=in_specs, out_specs=out_specs, check_vma=False
    )
```

```python
import functools
import math

import jax
import jax.numpy as jnp
from jax import lax
from jax.experimental import pallas as pl
from jax.experimental.pallas import tpu as pltpu
from jax.sharding import Mesh, PartitionSpec as P

D = 8192
BF16 = jnp.bfloat16
F32 = jnp.float32
REP = ("z", "x")
FSDP = ("y", "core")
VMEM = pl.BlockSpec(memory_space=pltpu.VMEM)
HBM = pl.BlockSpec(memory_space=pltpu.HBM)
MEGA = 1024 * 1024
CUTS = 4
PIECES = 2
MERGE_CUTS = 1
LANES = 128


def halves(x):
    high = x.astype(BF16)
    return high, (x - high.astype(F32)).astype(BF16)


def dot(left, right, dims):
    return lax.dot_general(left, right, (dims, ((), ())), preferred_element_type=F32)


def exact(left, right, dims):
    return lax.dot_general(
        left,
        right,
        (dims, ((), ())),
        precision=lax.Precision.HIGHEST,
        preferred_element_type=F32,
    )


def narrow(x, rank):
    return x[:rank] + x[rank : 2 * rank]


def stack(ref, value, lane):
    height, width = value.shape[0], value.shape[1] // CUTS
    for i in range(CUTS):
        ref[i * height : (i + 1) * height, lane : lane + width] = value[
            :, i * width : (i + 1) * width
        ]


def unstack(value):
    height = value.shape[0] // CUTS
    return jnp.concatenate(
        [value[i * height : (i + 1) * height] for i in range(CUTS)], axis=1
    )


def pack(ref, pair):
    for h, value in enumerate(pair):
        height = value.shape[0]
        for i in range(value.shape[1] // LANES):
            ref[i * height : (i + 1) * height, h * LANES : (h + 1) * LANES] = value[
                :, i * LANES : (i + 1) * LANES
            ]


def unpack(value, height):
    return [
        jnp.concatenate(
            [
                value[i : i + height, h * LANES : (h + 1) * LANES]
                for i in range(0, value.shape[0], height)
            ],
            axis=1,
        )
        for h in range(2)
    ]


def prepare(acts, grads_out, warm_q, out, here, w_rows, in_sems, out_sems):
    parts, height, rows = out.shape
    tokens = acts.shape[0]
    piece = height - tokens
    moves = [
        pltpu.make_async_copy(
            acts.at[:, pl.ds(i * rows, rows)], here.at[i], in_sems.at[i]
        )
        for i in range(parts)
    ]
    for move in moves:
        move.start()
    sends = []
    for i in range(parts):
        moves[i].wait()
        sends.append(
            pltpu.make_async_copy(
                here.at[i], out.at[i, pl.ds(0, tokens)], out_sems.at[i]
            )
        )
        sends[-1].start()
    rank, width = warm_q.shape[1:]
    per = rank // piece
    for k in range(2):
        left = jnp.concatenate(halves(warm_q[k]), axis=0)
        grads = grads_out[:, k * width : (k + 1) * width]
        w = narrow(dot(left, grads, ((1,), (1,))), rank)
        for half, value in enumerate(halves(w)):
            for b in range(per):
                at = (half * 2 * per + k * per + b) * tokens
                w_rows[:, at : at + tokens] = value[b * piece : (b + 1) * piece]
    for i in range(parts):
        sends.append(
            pltpu.make_async_copy(
                w_rows, out.at[i, pl.ds(tokens, piece)], out_sems.at[parts + i]
            )
        )
        sends[-1].start()
    for send in sends:
        send.wait()


def error_part(place, error, warm_q, out, given):
    given[...] = error[0, 1 - place[1]]
    rank = warm_q.shape[1]
    for k in range(2):
        left = jnp.concatenate(halves(warm_q[k]), axis=0)
        out[k * rank : (k + 1) * rank] = narrow(
            dot(left, error[0, k], ((1,), (1,))), rank
        )


def first_left(got, p_error, out, w):
    parts, height, _ = got.shape
    tokens = w.shape[1] // parts
    piece = height - tokens
    total = w.shape[0] // piece
    for s in range(parts):
        for b in range(total):
            w[b * piece : (b + 1) * piece, s * tokens : (s + 1) * tokens] = got[
                s, tokens:height, b * tokens : (b + 1) * tokens
            ]
    p = p_error[...]
    both = jnp.zeros((w.shape[0], got.shape[2]), F32)
    for s in range(0, parts, 2):
        x = jnp.concatenate([got[s, :tokens], got[s + 1, :tokens]], axis=0)
        both += dot(w[:, s * tokens : (s + 2) * tokens], x, ((1,), (0,)))
    p += narrow(both, p.shape[0])
    rank = p.shape[0] // 2
    pack(out, (p[:rank], p[rank:]))


def merge(place, got, got_other, error, error_other, *refs):
    blocks, outs, scratch = refs[:5], refs[5:9], refs[9:]
    x, d, e, high, low, d_sems, x_sems, e_sems, out_sems = scratch
    y, core = place[0], place[1]
    rows = e.shape[1]
    tokens = blocks[0].shape[0] // 2
    cut = rows // MERGE_CUTS
    d_moves, at = [], 0
    for i, block in enumerate(blocks):
        tall = block.shape[0]
        d_moves.append(
            pltpu.make_async_copy(block, d.at[pl.ds(at, tall)], d_sems.at[i])
        )
        at += tall
    x_moves, e_moves = [], []
    for h, source in enumerate((got, got_other)):
        for s in range(4):
            first = 2 * lax.rem(y + 4 - s, 4)
            for n, at in ((0, first + core), (1, first + 1 - core)):
                i = 2 * s + n
                x_moves.append(
                    pltpu.make_async_copy(
                        source.at[at, pl.ds(0, tokens)],
                        x.at[h, pl.ds(i * tokens, tokens)],
                        x_sems.at[8 * h + i],
                    )
                )
        for i in range(MERGE_CUTS):
            at = pl.ds(i * cut, cut)
            part = error_other.at[at] if h else error.at[0, core, at]
            e_moves.append(
                pltpu.make_async_copy(part, e.at[h, at], e_sems.at[MERGE_CUTS * h + i])
            )
    for move in (
        d_moves + x_moves[:8] + e_moves[:MERGE_CUTS] + x_moves[8:] + e_moves[MERGE_CUTS:]
    ):
        move.start()
    for move in d_moves:
        move.wait()
    sends = []
    for h in range(2):
        for move in x_moves[8 * h : 8 * h + 8]:
            move.wait()
        for i in range(MERGE_CUTS):
            n = MERGE_CUTS * h + i
            at = slice(i * cut, (i + 1) * cut)
            e_moves[n].wait()
            grad = dot(x[h, :, at], d[...], ((0,), (0,)))
            high[h, at], low[h, at] = halves(grad + e[h, at].astype(F32))
            for m, here in enumerate((high, low)):
                send = pltpu.make_async_copy(
                    here.at[h, at], outs[2 * h + m].at[at], out_sems.at[2 * n + m]
                )
                send.start()
                sends.append(send)
    for send in sends:
        send.wait()


def fetch(sources, high, low, sems):
    cut = high.shape[1] // PIECES
    moves = []
    for h in range(2):
        for i in range(PIECES):
            at = pl.ds(i * cut, cut)
            n = 2 * (PIECES * h + i)
            moves.append(
                [
                    pltpu.make_async_copy(
                        sources[2 * h].at[at], high.at[h, at], sems.at[n]
                    ),
                    pltpu.make_async_copy(
                        sources[2 * h + 1].at[at], low.at[h, at], sems.at[n + 1]
                    ),
                ]
            )
    for both in moves:
        for move in both:
            move.start()
    return moves


def multiply(left, high, low, dims):
    left_high, left_low = halves(left)
    both = jnp.concatenate([left_high, left_low], axis=0)
    return narrow(dot(both, high, dims), left.shape[0]) + dot(left_high, low, dims)


def right_factor(replicas, p_sum, *refs):
    sources, (p_mine, p_given, out, high, low, sems) = refs[:4], refs[4:]
    moves = fetch(sources, high, low, sems)
    p = [x / replicas for x in unpack(p_sum[...], p_mine.shape[0])]
    p_mine[...] = p[0]
    stack(p_given, p[1], 0)
    gram = q = 0.0
    for h in range(2):
        gram += exact(p[h], p[h], ((1,), (1,)))
    for h in range(2):
        for both in moves[PIECES * h : PIECES * (h + 1)]:
            for move in both:
                move.wait()
        q += multiply(p[h], high[h], low[h], ((1,), (0,)))
    stack(out, q, 0)
    stack(out, gram, q.shape[1] // CUTS)


def inverse_factors(grams):
    n = grams[0].shape[0]
    row = lax.broadcasted_iota(jnp.int32, (n, n), 0)
    column = lax.broadcasted_iota(jnp.int32, (n, n), 1)
    same = row == column
    one = same.astype(F32)
    below = lax.broadcasted_iota(jnp.int32, (n, 2 * n), 0)
    ts = [jnp.concatenate([gram, one], axis=1) for gram in grams]
    for j in range(n - 1):
        for i, t in enumerate(ts):
            pivot_row = t[j : j + 1] / t[j : j + 1, j : j + 1]
            factor = jnp.broadcast_to(t[:, j : j + 1], t.shape)
            ts[i] = t - jnp.where(below > j, factor, 0.0) * pivot_row
    inverses = []
    for t in ts:
        pivots = jnp.sum(jnp.where(same, t[:, :n], 0.0), axis=1, keepdims=True)
        inverses.append(t[:, n:] / jnp.sqrt(pivots))
    return inverses


def summed(sums, replicas, rank, width):
    last = (width + rank) // CUTS
    return (
        unstack(sums[:, : width // CUTS]) / replicas,
        unstack(sums[:, width // CUTS : last]) / replicas,
    )


def left_factor(replicas, rank, q_sum, *refs):
    sources, (out, high, low, sems) = refs[:4], refs[4:]
    moves = fetch(sources, high, low, sems)
    q, gram = summed(q_sum[...], replicas, rank, high.shape[2])
    (inverse,) = inverse_factors([gram])
    cut = high.shape[1] // PIECES
    p = []
    for n in range(2 * PIECES):
        for move in moves[n]:
            move.wait()
        h, i = divmod(n, PIECES)
        at = slice(i * cut, (i + 1) * cut)
        p.append(multiply(q, high[h, at], low[h, at], ((1,), (1,))))
    pair = [
        jnp.concatenate(p[PIECES * h : PIECES * (h + 1)], axis=1) for h in range(2)
    ]
    pack(out, [exact(inverse, x, ((1,), (0,))) for x in pair])


def finish(replicas, rank, place, q_mine, other, p_mine, *refs):
    sources, (new_error, p_factor, q_factor), scratch = refs[:4], refs[4:7], refs[7:]
    high, low, sems, out, out_sems, lefts, rights = scratch
    rows, width = high.shape[1:]
    moves = fetch(sources, high, low, sems)
    core = place[1]
    cut = rows // CUTS

    @pl.when(core >= 0)
    def _():
        sums = [
            summed(x, replicas, rank, width) for x in (q_mine[...], other[:, cut:])
        ]
        p_raws = (p_mine[...], unstack(other[:, :cut]))
        inverses = inverse_factors([gram for _, gram in sums])
        for n, p_raw in enumerate(p_raws):
            k = 1 - core if n else core
            q = exact(inverses[n], sums[n][0], ((1,), (0,)))
            q_factor[k] = q
            p_hat = exact(inverses[n], p_raw, ((1,), (0,)))
            p_factor[k] = p_hat * math.sqrt(D)
            p_high, p_low = halves(p_hat)
            q_high, q_low = halves(q)
            lefts[n] = jnp.concatenate([p_high, p_low, p_high, p_low], axis=0)
            rights[n] = jnp.concatenate([q_high, q_high, q_low, q_low], axis=0)
    sends = []
    for n in range(2):
        k = 1 - core if n else core
        for i in range(CUTS):
            if i % (CUTS // PIECES) == 0:
                for move in moves[PIECES * n + i * PIECES // CUTS]:
                    move.wait()
            at = slice(i * cut, (i + 1) * cut)
            approx = dot(lefts[n, :, at], rights[n], ((0,), (0,)))
            merged = high[n, at].astype(F32) + low[n, at].astype(F32)
            out[n, at] = (merged - approx).astype(BF16)
            send = pltpu.make_async_copy(
                out.at[n, at],
                new_error.at[0, k, pl.ds(i * cut, cut)],
                out_sems.at[CUTS * n + i],
            )
            send.start()
            sends.append(send)
    for send in sends:
        send.wait()


def call(kernel, outs, *args, space=52, cost=None, **kw):
    params = pltpu.CompilerParams(vmem_limit_bytes=space * MEGA)
    if cost is not None:
        kw["cost_estimate"] = pl.CostEstimate(
            flops=cost[0], bytes_accessed=cost[1], transcendentals=0
        )
    kw.setdefault("in_specs", [VMEM] * len(args))
    kw.setdefault("out_specs", [VMEM] * len(outs))
    return pl.pallas_call(kernel, out_shape=outs, compiler_params=params, **kw)(*args)


def array(shape, dtype):
    return jax.ShapeDtypeStruct(shape, dtype)


def swap(x, axis):
    return lax.all_to_all(x, axis, 0, 0, tiled=True)


def shared(x, axis):
    n = lax.axis_size(axis)
    return swap(x, axis).reshape(n, x.shape[0] // n, x.shape[1]).sum(0)


def copied(x, axis):
    everywhere = jnp.broadcast_to(x[None], (lax.axis_size(axis),) + x.shape)
    return swap(everywhere.reshape(-1, x.shape[1]), axis)


def total(x, axis):
    return copied(shared(x, axis), axis)


def total_everywhere(x):
    mine = shared(x, ("x", "y"))
    tall = mine.shape[0]
    mine = copied(mine, "z").reshape(-1, tall, mine.shape[1]).sum(0)
    return copied(mine, ("x", "y"))


def flip(x):
    return lax.ppermute(x, "core", [(0, 1), (1, 0)])


def on_device(acts, grads_out, error, warm_q):
    _, rank, width = warm_q.shape
    rows = error.shape[2]
    tokens = acts.shape[0]
    fsdp = lax.axis_size(FSDP)
    replicas = lax.axis_size(REP)
    piece = 4 * rank * tokens // rows
    pairs = 2 * rank

    (blocks,) = call(
        prepare,
        [array((fsdp, tokens + piece, rows), BF16)],
        acts,
        grads_out,
        warm_q,
        space=60,
        in_specs=[HBM, VMEM, VMEM],
        out_specs=[HBM],
        scratch_shapes=[
            pltpu.VMEM((fsdp, tokens, rows), BF16),
            pltpu.VMEM((piece, rows), BF16),
            pltpu.SemaphoreType.DMA((fsdp,)),
            pltpu.SemaphoreType.DMA((2 * fsdp,)),
        ],
    )
    got = swap(blocks, FSDP)

    core = lax.axis_index("core")
    place = jnp.stack([lax.axis_index("y"), core]).astype(jnp.int32)
    late_d, late_error, late_q, _ = lax.optimization_barrier(
        (grads_out, error, warm_q, blocks)
    )
    smem = pl.BlockSpec(memory_space=pltpu.SMEM)
    p_error, error_given = call(
        error_part,
        [array((pairs, rows), F32), array((rows, width), BF16)],
        place,
        late_error,
        late_q,
        in_specs=[smem, VMEM, VMEM],
        cost=(10**10, 10**8),
    )
    d_kept = lax.dynamic_slice_in_dim(late_d, core * width, width, 1)
    d_given = lax.dynamic_slice_in_dim(late_d, (1 - core) * width, width, 1)
    d_here = jnp.concatenate([d_kept, flip(d_given)], axis=0)
    d_here, p_error, got = lax.optimization_barrier((d_here, p_error, got))
    error_other = flip(error_given)

    up = [(i, (i + 1) % 4) for i in range(4)]
    down = [(i, (i + 3) % 4) for i in range(4)]
    d_up, d_down = lax.ppermute(d_here, "y", up), lax.ppermute(d_here, "y", down)
    got_other = flip(got)
    packed = array((rows // LANES * rank, 2 * LANES), F32)
    (p_part,) = call(
        first_left,
        [packed],
        got,
        p_error,
        space=16,
        scratch_shapes=[pltpu.VMEM((2 * pairs, fsdp * tokens), BF16)],
    )
    p_both = shared(p_part, REP)
    first, second = p_both[:, :LANES], p_both[:, LANES:]
    kept = jnp.where(core == 0, first, second)
    given = jnp.where(core == 0, second, first)
    p_piece, _, _ = lax.optimization_barrier(
        (jnp.concatenate([kept, flip(given)], axis=1), d_up, d_down)
    )
    far = [
        lax.ppermute(d_up[:tokens], "y", up),
        lax.ppermute(d_down[tokens:], "y", down),
    ]
    d = [d_here, d_up, *far, d_down]
    p_sum = copied(p_piece, REP)

    part = array((rows, width), BF16)
    local = [
        pltpu.VMEM((2, rows, width), BF16),
        pltpu.VMEM((2, rows, width), BF16),
        pltpu.SemaphoreType.DMA((4 * PIECES,)),
    ]
    merged = call(
        merge,
        [part] * 4,
        place,
        got,
        got_other,
        error,
        error_other,
        *d,
        in_specs=[smem] + [HBM] * 9,
        cost=(4*10**10, 2 * 10**7),
        out_specs=[HBM] * 4,
        scratch_shapes=[
            pltpu.VMEM((2, fsdp * tokens, rows), BF16),
            pltpu.VMEM((fsdp * tokens, width), BF16),
            pltpu.VMEM((2, rows, width), BF16),
            pltpu.VMEM((2, rows, width), BF16),
            pltpu.VMEM((2, rows, width), BF16),
            pltpu.SemaphoreType.DMA((5,)),
            pltpu.SemaphoreType.DMA((16,)),
            pltpu.SemaphoreType.DMA((2 * MERGE_CUTS,)),
            pltpu.SemaphoreType.DMA((4 * MERGE_CUTS,)),
        ],
    )
    high, low, high_given, low_given = merged

    def right(p_sum):
        *p_raw, sent = call(
            functools.partial(right_factor, replicas),
            [
                array((rank, rows), F32),
                array((CUTS * rank, rows // CUTS), F32),
                array((CUTS * rank, (width + rank) // CUTS), F32),
            ],
            p_sum,
            *merged,
            in_specs=[VMEM] + [HBM] * 4,
            scratch_shapes=local,
        )
        return p_raw, total_everywhere(sent)

    _, q_sum = right(p_sum)
    (p_part,) = call(
        functools.partial(left_factor, replicas, rank),
        [packed],
        q_sum,
        *merged,
        in_specs=[VMEM] + [HBM] * 4,
        scratch_shapes=local,
    )
    (p_mine, p_given), q_sum = right(total(p_part, REP))
    return call(
        functools.partial(finish, replicas, rank),
        [
            array((1, 2, rows, width), BF16),
            array((2, rank, rows), F32),
            array((2, rank, width), F32),
        ],
        place,
        q_sum,
        flip(jnp.concatenate([p_given, q_sum], axis=1)),
        p_mine,
        high,
        low,
        flip(high_given),
        flip(low_given),
        in_specs=[smem] + [VMEM] * 3 + [HBM] * 4,
        out_specs=[HBM, VMEM, VMEM],
        scratch_shapes=local
        + [
            pltpu.VMEM((2, rows, width), BF16),
            pltpu.SemaphoreType.DMA((2 * CUTS,)),
            pltpu.VMEM((2, 4 * rank, rows), BF16),
            pltpu.VMEM((2, 4 * rank, width), BF16),
        ],
    )


def solution(mesh):
    devices = mesh.devices.reshape(8, 4, 4, 2)
    torus = Mesh(devices, REP + FSDP)
    in_specs = (
        P(REP + FSDP, None),
        P(REP + FSDP, None),
        P(REP, None, FSDP, None),
        P(),
    )
    out_specs = (P(REP, None, FSDP, None), P(None, None, FSDP), P())
    return jax.shard_map(
        on_device, mesh=torus, in_specs=in_specs, out_specs=out_specs, check_vma=False
    )
```

```python
import functools
import math

import jax
import jax.numpy as jnp
from jax import lax
from jax.experimental import pallas as pl
from jax.experimental.pallas import tpu as pltpu
from jax.sharding import Mesh, PartitionSpec as P

D = 8192
BF16 = jnp.bfloat16
F32 = jnp.float32
REP = ("z", "x")
FSDP = ("y", "core")
VMEM = pl.BlockSpec(memory_space=pltpu.VMEM)
HBM = pl.BlockSpec(memory_space=pltpu.HBM)
MEGA = 1024 * 1024
CUTS = 4
PIECES = 2
MERGE_CUTS = 1
LANES = 128


def halves(x):
    high = x.astype(BF16)
    return high, (x - high.astype(F32)).astype(BF16)


def dot(left, right, dims):
    return lax.dot_general(left, right, (dims, ((), ())), preferred_element_type=F32)


def exact(left, right, dims):
    return lax.dot_general(
        left,
        right,
        (dims, ((), ())),
        precision=lax.Precision.HIGHEST,
        preferred_element_type=F32,
    )


def narrow(x, rank):
    return x[:rank] + x[rank : 2 * rank]


def stack(ref, value, lane):
    height, width = value.shape[0], value.shape[1] // CUTS
    for i in range(CUTS):
        ref[i * height : (i + 1) * height, lane : lane + width] = value[
            :, i * width : (i + 1) * width
        ]


def unstack(value):
    height = value.shape[0] // CUTS
    return jnp.concatenate(
        [value[i * height : (i + 1) * height] for i in range(CUTS)], axis=1
    )


def pack(ref, pair):
    for h, value in enumerate(pair):
        height = value.shape[0]
        for i in range(value.shape[1] // LANES):
            ref[i * height : (i + 1) * height, h * LANES : (h + 1) * LANES] = value[
                :, i * LANES : (i + 1) * LANES
            ]


def unpack(value, height):
    return [
        jnp.concatenate(
            [
                value[i : i + height, h * LANES : (h + 1) * LANES]
                for i in range(0, value.shape[0], height)
            ],
            axis=1,
        )
        for h in range(2)
    ]


def prepare(acts, grads_out, warm_q, out, here, w_rows, in_sems, out_sems):
    parts, height, rows = out.shape
    tokens = acts.shape[0]
    piece = height - tokens
    moves = [
        pltpu.make_async_copy(
            acts.at[:, pl.ds(i * rows, rows)], here.at[i], in_sems.at[i]
        )
        for i in range(parts)
    ]
    for move in moves:
        move.start()
    rank, width = warm_q.shape[1:]
    per = rank // piece
    for k in range(2):
        left = jnp.concatenate(halves(warm_q[k]), axis=0)
        grads = grads_out[:, k * width : (k + 1) * width]
        w = narrow(dot(left, grads, ((1,), (1,))), rank)
        for half, value in enumerate(halves(w)):
            for b in range(per):
                at = (half * 2 * per + k * per + b) * tokens
                w_rows[:, at : at + tokens] = value[b * piece : (b + 1) * piece]
    sends = []
    for i in range(parts):
        moves[i].wait()
        sends.append(
            pltpu.make_async_copy(
                here.at[i], out.at[i, pl.ds(0, tokens)], out_sems.at[i]
            )
        )
        sends[-1].start()
    for i in range(parts):
        sends.append(
            pltpu.make_async_copy(
                w_rows, out.at[i, pl.ds(tokens, piece)], out_sems.at[parts + i]
            )
        )
        sends[-1].start()
    for send in sends:
        send.wait()


def error_part(place, error, warm_q, out, given):
    given[...] = error[0, 1 - place[1]]
    rank = warm_q.shape[1]
    for k in range(2):
        left = jnp.concatenate(halves(warm_q[k]), axis=0)
        out[k * rank : (k + 1) * rank] = narrow(
            dot(left, error[0, k], ((1,), (1,))), rank
        )


def first_left(got, p_error, out, w):
    parts, height, _ = got.shape
    tokens = w.shape[1] // parts
    piece = height - tokens
    total = w.shape[0] // piece
    for s in range(parts):
        for b in range(total):
            w[b * piece : (b + 1) * piece, s * tokens : (s + 1) * tokens] = got[
                s, tokens:height, b * tokens : (b + 1) * tokens
            ]
    p = p_error[...]
    both = jnp.zeros((w.shape[0], got.shape[2]), F32)
    for s in range(0, parts, 2):
        x = jnp.concatenate([got[s, :tokens], got[s + 1, :tokens]], axis=0)
        both += dot(w[:, s * tokens : (s + 2) * tokens], x, ((1,), (0,)))
    p += narrow(both, p.shape[0])
    rank = p.shape[0] // 2
    pack(out, (p[:rank], p[rank:]))


def merge(place, got, got_other, error, error_other, *refs):
    blocks, outs, scratch = refs[:5], refs[5:9], refs[9:]
    x, d, e, high, low, d_sems, x_sems, e_sems, out_sems = scratch
    y, core = place[0], place[1]
    rows = e.shape[1]
    tokens = blocks[0].shape[0] // 2
    cut = rows // MERGE_CUTS
    d_moves, at = [], 0
    for i, block in enumerate(blocks):
        tall = block.shape[0]
        d_moves.append(
            pltpu.make_async_copy(block, d.at[pl.ds(at, tall)], d_sems.at[i])
        )
        at += tall
    x_moves, e_moves = [], []
    for h, source in enumerate((got, got_other)):
        for s in range(4):
            first = 2 * lax.rem(y + 4 - s, 4)
            for n, at in ((0, first + core), (1, first + 1 - core)):
                i = 2 * s + n
                x_moves.append(
                    pltpu.make_async_copy(
                        source.at[at, pl.ds(0, tokens)],
                        x.at[h, pl.ds(i * tokens, tokens)],
                        x_sems.at[8 * h + i],
                    )
                )
        for i in range(MERGE_CUTS):
            at = pl.ds(i * cut, cut)
            part = error_other.at[at] if h else error.at[0, core, at]
            e_moves.append(
                pltpu.make_async_copy(part, e.at[h, at], e_sems.at[MERGE_CUTS * h + i])
            )
    for move in (
        d_moves + x_moves[:8] + e_moves[:MERGE_CUTS] + x_moves[8:] + e_moves[MERGE_CUTS:]
    ):
        move.start()
    for move in d_moves:
        move.wait()
    sends = []
    for h in range(2):
        for move in x_moves[8 * h : 8 * h + 8]:
            move.wait()
        for i in range(MERGE_CUTS):
            n = MERGE_CUTS * h + i
            at = slice(i * cut, (i + 1) * cut)
            e_moves[n].wait()
            grad = dot(x[h, :, at], d[...], ((0,), (0,)))
            high[h, at], low[h, at] = halves(grad + e[h, at].astype(F32))
            for m, here in enumerate((high, low)):
                send = pltpu.make_async_copy(
                    here.at[h, at], outs[2 * h + m].at[at], out_sems.at[2 * n + m]
                )
                send.start()
                sends.append(send)
    for send in sends:
        send.wait()


def fetch(sources, high, low, sems):
    cut = high.shape[1] // PIECES
    moves = []
    for h in range(2):
        for i in range(PIECES):
            at = pl.ds(i * cut, cut)
            n = 2 * (PIECES * h + i)
            moves.append(
                [
                    pltpu.make_async_copy(
                        sources[2 * h].at[at], high.at[h, at], sems.at[n]
                    ),
                    pltpu.make_async_copy(
                        sources[2 * h + 1].at[at], low.at[h, at], sems.at[n + 1]
                    ),
                ]
            )
    for both in moves:
        for move in both:
            move.start()
    return moves


def multiply(left, high, low, dims):
    left_high, left_low = halves(left)
    both = jnp.concatenate([left_high, left_low], axis=0)
    return narrow(dot(both, high, dims), left.shape[0]) + dot(left_high, low, dims)


def right_factor(replicas, place, p_sum, *refs):
    sources, (p_mine, p_given, out, high, low, sems) = refs[:4], refs[4:]
    moves = fetch(sources, high, low, sems)

    @pl.when(place[1] >= 0)
    def _():
        p = [x / replicas for x in unpack(p_sum[...], p_mine.shape[0])]
        p_mine[...] = p[0]
        stack(p_given, p[1], 0)
        gram = exact(p[0], p[0], ((1,), (1,))) + exact(p[1], p[1], ((1,), (1,)))
        stack(out, gram, high.shape[2] // CUTS)

    q = 0.0
    for h, p in enumerate((p_mine[...], unstack(p_given[...]))):
        for both in moves[PIECES * h : PIECES * (h + 1)]:
            for move in both:
                move.wait()
        q += multiply(p, high[h], low[h], ((1,), (0,)))
    stack(out, q, 0)


def inverse_factors(grams):
    n = grams[0].shape[0]
    row = lax.broadcasted_iota(jnp.int32, (n, n), 0)
    column = lax.broadcasted_iota(jnp.int32, (n, n), 1)
    same = row == column
    one = same.astype(F32)
    below = lax.broadcasted_iota(jnp.int32, (n, 2 * n), 0)
    ts = [jnp.concatenate([gram, one], axis=1) for gram in grams]
    for j in range(n - 1):
        for i, t in enumerate(ts):
            pivot_row = t[j : j + 1] / t[j : j + 1, j : j + 1]
            factor = jnp.broadcast_to(t[:, j : j + 1], t.shape)
            ts[i] = t - jnp.where(below > j, factor, 0.0) * pivot_row
    inverses = []
    for t in ts:
        pivots = jnp.sum(jnp.where(same, t[:, :n], 0.0), axis=1, keepdims=True)
        inverses.append(t[:, n:] / jnp.sqrt(pivots))
    return inverses


def summed(sums, replicas, rank, width):
    last = (width + rank) // CUTS
    return (
        unstack(sums[:, : width // CUTS]) / replicas,
        unstack(sums[:, width // CUTS : last]) / replicas,
    )


def left_factor(replicas, rank, q_sum, *refs):
    sources, (out, high, low, sems) = refs[:4], refs[4:]
    moves = fetch(sources, high, low, sems)
    q, gram = summed(q_sum[...], replicas, rank, high.shape[2])
    (inverse,) = inverse_factors([gram])
    cut = high.shape[1] // PIECES
    p = []
    for n in range(2 * PIECES):
        for move in moves[n]:
            move.wait()
        h, i = divmod(n, PIECES)
        at = slice(i * cut, (i + 1) * cut)
        p.append(multiply(q, high[h, at], low[h, at], ((1,), (1,))))
    pair = [
        jnp.concatenate(p[PIECES * h : PIECES * (h + 1)], axis=1) for h in range(2)
    ]
    pack(out, [exact(inverse, x, ((1,), (0,))) for x in pair])


def finish(replicas, rank, place, q_mine, other, p_mine, *refs):
    sources, (new_error, p_factor, q_factor), scratch = refs[:4], refs[4:7], refs[7:]
    high, low, sems, out, out_sems, lefts, rights = scratch
    rows, width = high.shape[1:]
    moves = fetch(sources, high, low, sems)
    core = place[1]
    cut = rows // CUTS

    @pl.when(core >= 0)
    def _():
        sums = [
            summed(x, replicas, rank, width) for x in (q_mine[...], other[:, cut:])
        ]
        p_raws = (p_mine[...], unstack(other[:, :cut]))
        inverses = inverse_factors([gram for _, gram in sums])
        for n, p_raw in enumerate(p_raws):
            k = 1 - core if n else core
            q = exact(inverses[n], sums[n][0], ((1,), (0,)))
            q_factor[k] = q
            p_hat = exact(inverses[n], p_raw, ((1,), (0,)))
            p_factor[k] = p_hat * math.sqrt(D)
            p_high, p_low = halves(p_hat)
            q_high, q_low = halves(q)
            lefts[n] = jnp.concatenate([p_high, p_low, p_high, p_low], axis=0)
            rights[n] = jnp.concatenate([q_high, q_high, q_low, q_low], axis=0)
    sends = []
    for n in range(2):
        k = 1 - core if n else core
        for i in range(CUTS):
            if i % (CUTS // PIECES) == 0:
                for move in moves[PIECES * n + i * PIECES // CUTS]:
                    move.wait()
            at = slice(i * cut, (i + 1) * cut)
            approx = dot(lefts[n, :, at], rights[n], ((0,), (0,)))
            merged = high[n, at].astype(F32) + low[n, at].astype(F32)
            out[n, at] = (merged - approx).astype(BF16)
            send = pltpu.make_async_copy(
                out.at[n, at],
                new_error.at[0, k, pl.ds(i * cut, cut)],
                out_sems.at[CUTS * n + i],
            )
            send.start()
            sends.append(send)
    for send in sends:
        send.wait()


def call(kernel, outs, *args, space=52, cost=None, **kw):
    params = pltpu.CompilerParams(vmem_limit_bytes=space * MEGA)
    if cost is not None:
        kw["cost_estimate"] = pl.CostEstimate(
            flops=cost[0], bytes_accessed=cost[1], transcendentals=0
        )
    kw.setdefault("in_specs", [VMEM] * len(args))
    kw.setdefault("out_specs", [VMEM] * len(outs))
    return pl.pallas_call(kernel, out_shape=outs, compiler_params=params, **kw)(*args)


def array(shape, dtype):
    return jax.ShapeDtypeStruct(shape, dtype)


def swap(x, axis):
    return lax.all_to_all(x, axis, 0, 0, tiled=True)


def shared(x, axis):
    n = lax.axis_size(axis)
    return swap(x, axis).reshape(n, x.shape[0] // n, x.shape[1]).sum(0)


def copied(x, axis):
    everywhere = jnp.broadcast_to(x[None], (lax.axis_size(axis),) + x.shape)
    return swap(everywhere.reshape(-1, x.shape[1]), axis)


def total(x, axis):
    return copied(shared(x, axis), axis)


def total_everywhere(x):
    mine = shared(x, ("x", "y"))
    tall = mine.shape[0]
    mine = copied(mine, "z").reshape(-1, tall, mine.shape[1]).sum(0)
    return copied(mine, ("x", "y"))


def flip(x):
    return lax.ppermute(x, "core", [(0, 1), (1, 0)])


def on_device(acts, grads_out, error, warm_q):
    _, rank, width = warm_q.shape
    rows = error.shape[2]
    tokens = acts.shape[0]
    fsdp = lax.axis_size(FSDP)
    replicas = lax.axis_size(REP)
    piece = 4 * rank * tokens // rows
    pairs = 2 * rank

    (blocks,) = call(
        prepare,
        [array((fsdp, tokens + piece, rows), BF16)],
        acts,
        grads_out,
        warm_q,
        space=60,
        in_specs=[HBM, VMEM, VMEM],
        out_specs=[HBM],
        scratch_shapes=[
            pltpu.VMEM((fsdp, tokens, rows), BF16),
            pltpu.VMEM((piece, rows), BF16),
            pltpu.SemaphoreType.DMA((fsdp,)),
            pltpu.SemaphoreType.DMA((2 * fsdp,)),
        ],
    )
    got = swap(blocks, FSDP)

    core = lax.axis_index("core")
    place = jnp.stack([lax.axis_index("y"), core]).astype(jnp.int32)
    late_d, late_error, late_q, _ = lax.optimization_barrier(
        (grads_out, error, warm_q, blocks)
    )
    smem = pl.BlockSpec(memory_space=pltpu.SMEM)
    p_error, error_given = call(
        error_part,
        [array((pairs, rows), F32), array((rows, width), BF16)],
        place,
        late_error,
        late_q,
        in_specs=[smem, VMEM, VMEM],
        cost=(10**10, 10**8),
    )
    d_kept = lax.dynamic_slice_in_dim(late_d, core * width, width, 1)
    d_given = lax.dynamic_slice_in_dim(late_d, (1 - core) * width, width, 1)
    d_here = jnp.concatenate([d_kept, flip(d_given)], axis=0)
    d_here, p_error, got = lax.optimization_barrier((d_here, p_error, got))
    error_other = flip(error_given)

    up = [(i, (i + 1) % 4) for i in range(4)]
    down = [(i, (i + 3) % 4) for i in range(4)]
    d_up, d_down = lax.ppermute(d_here, "y", up), lax.ppermute(d_here, "y", down)
    got_other = flip(got)
    packed = array((rows // LANES * rank, 2 * LANES), F32)
    (p_part,) = call(
        first_left,
        [packed],
        got,
        p_error,
        space=16,
        scratch_shapes=[pltpu.VMEM((2 * pairs, fsdp * tokens), BF16)],
    )
    p_both = shared(p_part, REP)
    first, second = p_both[:, :LANES], p_both[:, LANES:]
    kept = jnp.where(core == 0, first, second)
    given = jnp.where(core == 0, second, first)
    p_piece, _, _ = lax.optimization_barrier(
        (jnp.concatenate([kept, flip(given)], axis=1), d_up, d_down)
    )
    far = [
        lax.ppermute(d_up[:tokens], "y", up),
        lax.ppermute(d_down[tokens:], "y", down),
    ]
    d = [d_here, d_up, *far, d_down]
    p_sum = copied(p_piece, REP)

    part = array((rows, width), BF16)
    local = [
        pltpu.VMEM((2, rows, width), BF16),
        pltpu.VMEM((2, rows, width), BF16),
        pltpu.SemaphoreType.DMA((4 * PIECES,)),
    ]
    merged = call(
        merge,
        [part] * 4,
        place,
        got,
        got_other,
        error,
        error_other,
        *d,
        in_specs=[smem] + [HBM] * 9,
        cost=(4*10**10, 2 * 10**7),
        out_specs=[HBM] * 4,
        scratch_shapes=[
            pltpu.VMEM((2, fsdp * tokens, rows), BF16),
            pltpu.VMEM((fsdp * tokens, width), BF16),
            pltpu.VMEM((2, rows, width), BF16),
            pltpu.VMEM((2, rows, width), BF16),
            pltpu.VMEM((2, rows, width), BF16),
            pltpu.SemaphoreType.DMA((5,)),
            pltpu.SemaphoreType.DMA((16,)),
            pltpu.SemaphoreType.DMA((2 * MERGE_CUTS,)),
            pltpu.SemaphoreType.DMA((4 * MERGE_CUTS,)),
        ],
    )
    high, low, high_given, low_given = merged

    def right(p_sum):
        *p_raw, sent = call(
            functools.partial(right_factor, replicas),
            [
                array((rank, rows), F32),
                array((CUTS * rank, rows // CUTS), F32),
                array((CUTS * rank, (width + rank) // CUTS), F32),
            ],
            place,
            p_sum,
            *merged,
            in_specs=[smem, VMEM] + [HBM] * 4,
            scratch_shapes=local,
        )
        return p_raw, total_everywhere(sent)

    _, q_sum = right(p_sum)
    (p_part,) = call(
        functools.partial(left_factor, replicas, rank),
        [packed],
        q_sum,
        *merged,
        in_specs=[VMEM] + [HBM] * 4,
        scratch_shapes=local,
    )
    (p_mine, p_given), q_sum = right(total(p_part, REP))
    return call(
        functools.partial(finish, replicas, rank),
        [
            array((1, 2, rows, width), BF16),
            array((2, rank, rows), F32),
            array((2, rank, width), F32),
        ],
        place,
        q_sum,
        flip(jnp.concatenate([p_given, q_sum], axis=1)),
        p_mine,
        high,
        low,
        flip(high_given),
        flip(low_given),
        in_specs=[smem] + [VMEM] * 3 + [HBM] * 4,
        out_specs=[HBM, VMEM, VMEM],
        scratch_shapes=local
        + [
            pltpu.VMEM((2, rows, width), BF16),
            pltpu.SemaphoreType.DMA((2 * CUTS,)),
            pltpu.VMEM((2, 4 * rank, rows), BF16),
            pltpu.VMEM((2, 4 * rank, width), BF16),
        ],
    )


def solution(mesh):
    devices = mesh.devices.reshape(8, 4, 4, 2)
    torus = Mesh(devices, REP + FSDP)
    in_specs = (
        P(REP + FSDP, None),
        P(REP + FSDP, None),
        P(REP, None, FSDP, None),
        P(),
    )
    out_specs = (P(REP, None, FSDP, None), P(None, None, FSDP), P())
    return jax.shard_map(
        on_device, mesh=torus, in_specs=in_specs, out_specs=out_specs, check_vma=False
    )
```

```python
import functools
import math

import jax
import jax.numpy as jnp
from jax import lax
from jax.experimental import pallas as pl
from jax.experimental.pallas import tpu as pltpu
from jax.sharding import Mesh, PartitionSpec as P

D = 8192
BF16 = jnp.bfloat16
F32 = jnp.float32
REP = ("z", "x")
FSDP = ("y", "core")
VMEM = pl.BlockSpec(memory_space=pltpu.VMEM)
HBM = pl.BlockSpec(memory_space=pltpu.HBM)
MEGA = 1024 * 1024
CUTS = 4
PIECES = 4
MERGE_CUTS = 1
LANES = 128


def halves(x):
    high = x.astype(BF16)
    return high, (x - high.astype(F32)).astype(BF16)


def dot(left, right, dims):
    return lax.dot_general(left, right, (dims, ((), ())), preferred_element_type=F32)


def exact(left, right, dims):
    return lax.dot_general(
        left,
        right,
        (dims, ((), ())),
        precision=lax.Precision.HIGHEST,
        preferred_element_type=F32,
    )


def narrow(x, rank):
    return x[:rank] + x[rank : 2 * rank]


def stack(ref, value, lane):
    height, width = value.shape[0], value.shape[1] // CUTS
    for i in range(CUTS):
        ref[i * height : (i + 1) * height, lane : lane + width] = value[
            :, i * width : (i + 1) * width
        ]


def unstack(value):
    height = value.shape[0] // CUTS
    return jnp.concatenate(
        [value[i * height : (i + 1) * height] for i in range(CUTS)], axis=1
    )


def pack(ref, pair):
    for h, value in enumerate(pair):
        height = value.shape[0]
        for i in range(value.shape[1] // LANES):
            ref[i * height : (i + 1) * height, h * LANES : (h + 1) * LANES] = value[
                :, i * LANES : (i + 1) * LANES
            ]


def unpack(value, height):
    return [
        jnp.concatenate(
            [
                value[i : i + height, h * LANES : (h + 1) * LANES]
                for i in range(0, value.shape[0], height)
            ],
            axis=1,
        )
        for h in range(2)
    ]


def prepare(acts, grads_out, warm_q, out, here, w_rows, in_sems, out_sems):
    parts, height, rows = out.shape
    tokens = acts.shape[0]
    piece = height - tokens
    moves = [
        pltpu.make_async_copy(
            acts.at[:, pl.ds(i * rows, rows)], here.at[i], in_sems.at[i]
        )
        for i in range(parts)
    ]
    for move in moves:
        move.start()
    rank, width = warm_q.shape[1:]
    per = rank // piece
    for k in range(2):
        left = jnp.concatenate(halves(warm_q[k]), axis=0)
        grads = grads_out[:, k * width : (k + 1) * width]
        w = narrow(dot(left, grads, ((1,), (1,))), rank)
        for half, value in enumerate(halves(w)):
            for b in range(per):
                at = (half * 2 * per + k * per + b) * tokens
                w_rows[:, at : at + tokens] = value[b * piece : (b + 1) * piece]
    sends = []
    for i in range(parts):
        moves[i].wait()
        sends.append(
            pltpu.make_async_copy(
                here.at[i], out.at[i, pl.ds(0, tokens)], out_sems.at[i]
            )
        )
        sends[-1].start()
    for i in range(parts):
        sends.append(
            pltpu.make_async_copy(
                w_rows, out.at[i, pl.ds(tokens, piece)], out_sems.at[parts + i]
            )
        )
        sends[-1].start()
    for send in sends:
        send.wait()


def error_part(place, error, warm_q, out, given):
    given[...] = error[0, 1 - place[1]]
    rank = warm_q.shape[1]
    for k in range(2):
        left = jnp.concatenate(halves(warm_q[k]), axis=0)
        out[k * rank : (k + 1) * rank] = narrow(
            dot(left, error[0, k], ((1,), (1,))), rank
        )


def first_left(got, p_error, out, w):
    parts, height, _ = got.shape
    tokens = w.shape[1] // parts
    piece = height - tokens
    total = w.shape[0] // piece
    for s in range(parts):
        for b in range(total):
            w[b * piece : (b + 1) * piece, s * tokens : (s + 1) * tokens] = got[
                s, tokens:height, b * tokens : (b + 1) * tokens
            ]
    p = p_error[...]
    both = jnp.zeros((w.shape[0], got.shape[2]), F32)
    for s in range(0, parts, 2):
        x = jnp.concatenate([got[s, :tokens], got[s + 1, :tokens]], axis=0)
        both += dot(w[:, s * tokens : (s + 2) * tokens], x, ((1,), (0,)))
    p += narrow(both, p.shape[0])
    rank = p.shape[0] // 2
    pack(out, (p[:rank], p[rank:]))


def merge(place, got, got_other, error, error_other, *refs):
    blocks, outs, scratch = refs[:5], refs[5:9], refs[9:]
    x, d, e, high, low, d_sems, x_sems, e_sems, out_sems = scratch
    y, core = place[0], place[1]
    rows = e.shape[1]
    tokens = blocks[0].shape[0] // 2
    cut = rows // MERGE_CUTS
    d_moves, at = [], 0
    for i, block in enumerate(blocks):
        tall = block.shape[0]
        d_moves.append(
            pltpu.make_async_copy(block, d.at[pl.ds(at, tall)], d_sems.at[i])
        )
        at += tall
    x_moves, e_moves = [], []
    for h, source in enumerate((got, got_other)):
        for s in range(4):
            first = 2 * lax.rem(y + 4 - s, 4)
            for n, at in ((0, first + core), (1, first + 1 - core)):
                i = 2 * s + n
                x_moves.append(
                    pltpu.make_async_copy(
                        source.at[at, pl.ds(0, tokens)],
                        x.at[h, pl.ds(i * tokens, tokens)],
                        x_sems.at[8 * h + i],
                    )
                )
        for i in range(MERGE_CUTS):
            at = pl.ds(i * cut, cut)
            part = error_other.at[at] if h else error.at[0, core, at]
            e_moves.append(
                pltpu.make_async_copy(part, e.at[h, at], e_sems.at[MERGE_CUTS * h + i])
            )
    for move in (
        d_moves + x_moves[:8] + e_moves[:MERGE_CUTS] + x_moves[8:] + e_moves[MERGE_CUTS:]
    ):
        move.start()
    for move in d_moves:
        move.wait()
    sends = []
    for h in range(2):
        for move in x_moves[8 * h : 8 * h + 8]:
            move.wait()
        for i in range(MERGE_CUTS):
            n = MERGE_CUTS * h + i
            at = slice(i * cut, (i + 1) * cut)
            e_moves[n].wait()
            grad = dot(x[h, :, at], d[...], ((0,), (0,)))
            high[h, at], low[h, at] = halves(grad + e[h, at].astype(F32))
            for m, here in enumerate((high, low)):
                send = pltpu.make_async_copy(
                    here.at[h, at], outs[2 * h + m].at[at], out_sems.at[2 * n + m]
                )
                send.start()
                sends.append(send)
    for send in sends:
        send.wait()


def fetch(sources, high, low, sems):
    cut = high.shape[1] // PIECES
    moves = []
    for h in range(2):
        for i in range(PIECES):
            at = pl.ds(i * cut, cut)
            n = 2 * (PIECES * h + i)
            moves.append(
                [
                    pltpu.make_async_copy(
                        sources[2 * h].at[at], high.at[h, at], sems.at[n]
                    ),
                    pltpu.make_async_copy(
                        sources[2 * h + 1].at[at], low.at[h, at], sems.at[n + 1]
                    ),
                ]
            )
    for both in moves:
        for move in both:
            move.start()
    return moves


def multiply(left, high, low, dims):
    left_high, left_low = halves(left)
    both = jnp.concatenate([left_high, left_low], axis=0)
    return narrow(dot(both, high, dims), left.shape[0]) + dot(left_high, low, dims)


def right_factor(replicas, place, p_sum, *refs):
    sources, (p_mine, p_given, out, high, low, sems) = refs[:4], refs[4:]
    moves = fetch(sources, high, low, sems)

    @pl.when(place[1] >= 0)
    def _():
        p = [x / replicas for x in unpack(p_sum[...], p_mine.shape[0])]
        p_mine[...] = p[0]
        stack(p_given, p[1], 0)
        gram = exact(p[0], p[0], ((1,), (1,))) + exact(p[1], p[1], ((1,), (1,)))
        stack(out, gram, high.shape[2] // CUTS)

    q = 0.0
    for h, p in enumerate((p_mine[...], unstack(p_given[...]))):
        for both in moves[PIECES * h : PIECES * (h + 1)]:
            for move in both:
                move.wait()
        q += multiply(p, high[h], low[h], ((1,), (0,)))
    stack(out, q, 0)


def inverse_factors(grams):
    n = grams[0].shape[0]
    row = lax.broadcasted_iota(jnp.int32, (n, n), 0)
    column = lax.broadcasted_iota(jnp.int32, (n, n), 1)
    same = row == column
    one = same.astype(F32)
    below = lax.broadcasted_iota(jnp.int32, (n, 2 * n), 0)
    ts = [jnp.concatenate([gram, one], axis=1) for gram in grams]
    for j in range(n - 1):
        for i, t in enumerate(ts):
            pivot_row = t[j : j + 1] / t[j : j + 1, j : j + 1]
            factor = jnp.broadcast_to(t[:, j : j + 1], t.shape)
            ts[i] = t - jnp.where(below > j, factor, 0.0) * pivot_row
    inverses = []
    for t in ts:
        pivots = jnp.sum(jnp.where(same, t[:, :n], 0.0), axis=1, keepdims=True)
        inverses.append(t[:, n:] / jnp.sqrt(pivots))
    return inverses


def summed(sums, replicas, rank, width):
    last = (width + rank) // CUTS
    return (
        unstack(sums[:, : width // CUTS]) / replicas,
        unstack(sums[:, width // CUTS : last]) / replicas,
    )


def left_factor(replicas, rank, q_sum, *refs):
    sources, (out, high, low, sems) = refs[:4], refs[4:]
    moves = fetch(sources, high, low, sems)
    q, gram = summed(q_sum[...], replicas, rank, high.shape[2])
    (inverse,) = inverse_factors([gram])
    cut = high.shape[1] // PIECES
    p = []
    for n in range(2 * PIECES):
        for move in moves[n]:
            move.wait()
        h, i = divmod(n, PIECES)
        at = slice(i * cut, (i + 1) * cut)
        p.append(multiply(q, high[h, at], low[h, at], ((1,), (1,))))
    pair = [
        jnp.concatenate(p[PIECES * h : PIECES * (h + 1)], axis=1) for h in range(2)
    ]
    pack(out, [exact(inverse, x, ((1,), (0,))) for x in pair])


def finish(replicas, rank, place, q_mine, other, p_mine, *refs):
    sources, (new_error, p_factor, q_factor), scratch = refs[:4], refs[4:7], refs[7:]
    high, low, sems, out, out_sems, lefts, rights = scratch
    rows, width = high.shape[1:]
    moves = fetch(sources, high, low, sems)
    core = place[1]
    cut = rows // CUTS

    @pl.when(core >= 0)
    def _():
        sums = [
            summed(x, replicas, rank, width) for x in (q_mine[...], other[:, cut:])
        ]
        p_raws = (p_mine[...], unstack(other[:, :cut]))
        inverses = inverse_factors([gram for _, gram in sums])
        for n, p_raw in enumerate(p_raws):
            k = 1 - core if n else core
            q = exact(inverses[n], sums[n][0], ((1,), (0,)))
            q_factor[k] = q
            p_hat = exact(inverses[n], p_raw, ((1,), (0,)))
            p_factor[k] = p_hat * math.sqrt(D)
            p_high, p_low = halves(p_hat)
            q_high, q_low = halves(q)
            lefts[n] = jnp.concatenate([p_high, p_low, p_high, p_low], axis=0)
            rights[n] = jnp.concatenate([q_high, q_high, q_low, q_low], axis=0)
    sends = []
    for n in range(2):
        k = 1 - core if n else core
        for i in range(CUTS):
            if i % (CUTS // PIECES) == 0:
                for move in moves[PIECES * n + i * PIECES // CUTS]:
                    move.wait()
            at = slice(i * cut, (i + 1) * cut)
            approx = dot(lefts[n, :, at], rights[n], ((0,), (0,)))
            merged = high[n, at].astype(F32) + low[n, at].astype(F32)
            out[n, at] = (merged - approx).astype(BF16)
            send = pltpu.make_async_copy(
                out.at[n, at],
                new_error.at[0, k, pl.ds(i * cut, cut)],
                out_sems.at[CUTS * n + i],
            )
            send.start()
            sends.append(send)
    for send in sends:
        send.wait()


def call(kernel, outs, *args, space=52, cost=None, **kw):
    params = pltpu.CompilerParams(vmem_limit_bytes=space * MEGA)
    if cost is not None:
        kw["cost_estimate"] = pl.CostEstimate(
            flops=cost[0], bytes_accessed=cost[1], transcendentals=0
        )
    kw.setdefault("in_specs", [VMEM] * len(args))
    kw.setdefault("out_specs", [VMEM] * len(outs))
    return pl.pallas_call(kernel, out_shape=outs, compiler_params=params, **kw)(*args)


def array(shape, dtype):
    return jax.ShapeDtypeStruct(shape, dtype)


def swap(x, axis):
    return lax.all_to_all(x, axis, 0, 0, tiled=True)


def shared(x, axis):
    n = lax.axis_size(axis)
    return swap(x, axis).reshape(n, x.shape[0] // n, x.shape[1]).sum(0)


def copied(x, axis):
    everywhere = jnp.broadcast_to(x[None], (lax.axis_size(axis),) + x.shape)
    return swap(everywhere.reshape(-1, x.shape[1]), axis)


def total(x, axis):
    return copied(shared(x, axis), axis)


def total_everywhere(x):
    mine = shared(x, ("x", "y"))
    tall = mine.shape[0]
    mine = copied(mine, "z").reshape(-1, tall, mine.shape[1]).sum(0)
    return copied(mine, ("x", "y"))


def flip(x):
    return lax.ppermute(x, "core", [(0, 1), (1, 0)])


def on_device(acts, grads_out, error, warm_q):
    _, rank, width = warm_q.shape
    rows = error.shape[2]
    tokens = acts.shape[0]
    fsdp = lax.axis_size(FSDP)
    replicas = lax.axis_size(REP)
    piece = 4 * rank * tokens // rows
    pairs = 2 * rank

    (blocks,) = call(
        prepare,
        [array((fsdp, tokens + piece, rows), BF16)],
        acts,
        grads_out,
        warm_q,
        space=60,
        in_specs=[HBM, VMEM, VMEM],
        out_specs=[HBM],
        scratch_shapes=[
            pltpu.VMEM((fsdp, tokens, rows), BF16),
            pltpu.VMEM((piece, rows), BF16),
            pltpu.SemaphoreType.DMA((fsdp,)),
            pltpu.SemaphoreType.DMA((2 * fsdp,)),
        ],
    )
    got = swap(blocks, FSDP)

    core = lax.axis_index("core")
    place = jnp.stack([lax.axis_index("y"), core]).astype(jnp.int32)
    late_d, late_error, late_q, _ = lax.optimization_barrier(
        (grads_out, error, warm_q, blocks)
    )
    smem = pl.BlockSpec(memory_space=pltpu.SMEM)
    p_error, error_given = call(
        error_part,
        [array((pairs, rows), F32), array((rows, width), BF16)],
        place,
        late_error,
        late_q,
        in_specs=[smem, VMEM, VMEM],
        cost=(10**10, 10**8),
    )
    d_kept = lax.dynamic_slice_in_dim(late_d, core * width, width, 1)
    d_given = lax.dynamic_slice_in_dim(late_d, (1 - core) * width, width, 1)
    d_here = jnp.concatenate([d_kept, flip(d_given)], axis=0)
    d_here, p_error, got = lax.optimization_barrier((d_here, p_error, got))
    error_other = flip(error_given)

    up = [(i, (i + 1) % 4) for i in range(4)]
    down = [(i, (i + 3) % 4) for i in range(4)]
    d_up, d_down = lax.ppermute(d_here, "y", up), lax.ppermute(d_here, "y", down)
    got_other = flip(got)
    packed = array((rows // LANES * rank, 2 * LANES), F32)
    (p_part,) = call(
        first_left,
        [packed],
        got,
        p_error,
        space=16,
        scratch_shapes=[pltpu.VMEM((2 * pairs, fsdp * tokens), BF16)],
    )
    p_both = shared(p_part, REP)
    first, second = p_both[:, :LANES], p_both[:, LANES:]
    kept = jnp.where(core == 0, first, second)
    given = jnp.where(core == 0, second, first)
    p_piece, _, _ = lax.optimization_barrier(
        (jnp.concatenate([kept, flip(given)], axis=1), d_up, d_down)
    )
    far = [
        lax.ppermute(d_up[:tokens], "y", up),
        lax.ppermute(d_down[tokens:], "y", down),
    ]
    d = [d_here, d_up, *far, d_down]
    p_sum = copied(p_piece, REP)

    part = array((rows, width), BF16)
    local = [
        pltpu.VMEM((2, rows, width), BF16),
        pltpu.VMEM((2, rows, width), BF16),
        pltpu.SemaphoreType.DMA((4 * PIECES,)),
    ]
    merged = call(
        merge,
        [part] * 4,
        place,
        got,
        got_other,
        error,
        error_other,
        *d,
        in_specs=[smem] + [HBM] * 9,
        cost=(4*10**10, 2 * 10**7),
        out_specs=[HBM] * 4,
        scratch_shapes=[
            pltpu.VMEM((2, fsdp * tokens, rows), BF16),
            pltpu.VMEM((fsdp * tokens, width), BF16),
            pltpu.VMEM((2, rows, width), BF16),
            pltpu.VMEM((2, rows, width), BF16),
            pltpu.VMEM((2, rows, width), BF16),
            pltpu.SemaphoreType.DMA((5,)),
            pltpu.SemaphoreType.DMA((16,)),
            pltpu.SemaphoreType.DMA((2 * MERGE_CUTS,)),
            pltpu.SemaphoreType.DMA((4 * MERGE_CUTS,)),
        ],
    )
    high, low, high_given, low_given = merged

    def right(p_sum):
        *p_raw, sent = call(
            functools.partial(right_factor, replicas),
            [
                array((rank, rows), F32),
                array((CUTS * rank, rows // CUTS), F32),
                array((CUTS * rank, (width + rank) // CUTS), F32),
            ],
            place,
            p_sum,
            *merged,
            in_specs=[smem, VMEM] + [HBM] * 4,
            scratch_shapes=local,
        )
        return p_raw, total_everywhere(sent)

    _, q_sum = right(p_sum)
    (p_part,) = call(
        functools.partial(left_factor, replicas, rank),
        [packed],
        q_sum,
        *merged,
        in_specs=[VMEM] + [HBM] * 4,
        scratch_shapes=local,
    )
    (p_mine, p_given), q_sum = right(total(p_part, REP))
    return call(
        functools.partial(finish, replicas, rank),
        [
            array((1, 2, rows, width), BF16),
            array((2, rank, rows), F32),
            array((2, rank, width), F32),
        ],
        place,
        q_sum,
        flip(jnp.concatenate([p_given, q_sum], axis=1)),
        p_mine,
        high,
        low,
        flip(high_given),
        flip(low_given),
        in_specs=[smem] + [VMEM] * 3 + [HBM] * 4,
        out_specs=[HBM, VMEM, VMEM],
        scratch_shapes=local
        + [
            pltpu.VMEM((2, rows, width), BF16),
            pltpu.SemaphoreType.DMA((2 * CUTS,)),
            pltpu.VMEM((2, 4 * rank, rows), BF16),
            pltpu.VMEM((2, 4 * rank, width), BF16),
        ],
    )


def solution(mesh):
    devices = mesh.devices.reshape(8, 4, 4, 2)
    torus = Mesh(devices, REP + FSDP)
    in_specs = (
        P(REP + FSDP, None),
        P(REP + FSDP, None),
        P(REP, None, FSDP, None),
        P(),
    )
    out_specs = (P(REP, None, FSDP, None), P(None, None, FSDP), P())
    return jax.shard_map(
        on_device, mesh=torus, in_specs=in_specs, out_specs=out_specs, check_vma=False
    )
```
